1024 devices in a mesh: blk: 128 (over x_hi, z, y), tower: 8 (over x_lo, core).
Axes of the slice: x: 8 (x_hi: 2, x_lo: 4; x = x_hi * 4 + x_lo), y: 8, z: 8, core: 2. Of those that a mesh axis runs over, the one named last changes fastest.
Arguments:
- image_embed: bfloat16 [16384, 1152], P('blk'), may hold values from -0.19921875 to 0.19921875
- text_embed: bfloat16 [16384, 1152], P(('blk', 'tower')), may hold values from -0.19921875 to 0.19921875
- image_feat: bfloat16 [16384, 6144], P('blk', 'tower'), may hold values from -0.75 to 0.75
- head: bfloat16 [1152, 6144], P(None, 'tower'), may hold values from -0.078125 to 0.078125
- sample_id: int32 [16384], P('blk'), may hold values from 0 to 4095
- domain: int32 [16384], P('blk'), may hold values from 0 to 7
- domain_bias: float32 [8], replicated, may hold values from -6 to -1
Outputs:
- image_grad: bfloat16 [16384, 6144], P('blk', 'tower')
- text_grad: float32 [16384, 1152], P(('blk', 'tower'))
- head_grad: float32 [1152, 6144], P('blk', 'tower')
The draws below stay inside these ranges and needn't reach their ends.
All inputs are finite; a program needn't handle non-finite values.
Results may differ from the reference program's by a relative error of at most 0.007.
Values may be sent and summed in bfloat16 or wider, within the bound.
No kernel may reach another device: no remote copies, remote signals or barrier semaphores. Data moves between devices by JAX's collectives and lax.ppermute only.
A program may use at most 32 MiB of HBM per device.

```python
import math
import jax
import jax.numpy as jnp
import numpy as np
from jax import lax

D = 1152
E = 6144
STEPS = 4
DOMAINS = 8
B_BLK = 128
IMAGES = 16384
N_BLK = 128


def with_ends(drawn, rng, smallest, top_value):
    spot = [jax.random.randint(jax.random.fold_in(rng, axis), (), 0, length) for axis, length in enumerate(drawn.shape)]
    longest = drawn.shape.index(max(drawn.shape))
    next_to = spot[:longest] + [(spot[longest] + 1) % drawn.shape[longest]] + spot[longest + 1:]
    return drawn.at[tuple(spot)].set(smallest).at[tuple(next_to)].set(top_value)


def level_of(stream_key, dims, cuts, least, top_value):
    level, own = 1.0, jax.random.fold_in(stream_key, 6)
    for dim, blocks in cuts:
        heights = jnp.exp(jax.random.uniform(jax.random.fold_in(own, dim), (blocks,), jnp.float32, least / len(cuts), top_value / len(cuts)))
        level = level * jnp.repeat(heights, dims[dim] // blocks).reshape([-1 if axis == dim else 1 for axis in range(len(dims))])
    return level


def rank_bounds(count, slope):
    weights = [(1 << 20) // math.isqrt(rank ** slope) + 1 for rank in range(1, count + 1)]
    deviation = 1 + sum(weights) // (1 << 30)
    return np.cumsum(np.array([max(1, weight // deviation) for weight in weights]))


def ranked_ids(key, shape, amount, lean):
    listing = rank_bounds(amount, lean)
    pick = jax.random.randint(jax.random.fold_in(key, 1), shape, 0, int(listing[amount - 1]))
    rank = jnp.searchsorted(jnp.asarray(listing, jnp.int32), pick, side="right")
    return jax.random.permutation(jax.random.fold_in(key, 2), amount)[rank].astype(jnp.int32)


def gaussian(own_key, shape, width, most, split=(), kind=jnp.bfloat16):
    gain = level_of(own_key, shape, split, -0.22, 0.18) if split else 1.0
    values = jax.random.normal(own_key, shape, jnp.float32) * width * gain
    return jnp.minimum(jnp.maximum(values, -most), most).astype(kind)


def setup_inputs(seed: int = 0) -> dict:
    seeds = jax.random.split(jax.random.key(seed), 8)
    return {
        "image_embed": gaussian(seeds[0], (IMAGES, D), 0.03, 0.19921875, ((0, 128),)),
        "text_embed": gaussian(seeds[1], (IMAGES, D), 0.03, 0.19921875, ((0, 1024),)),
        "image_feat": gaussian(seeds[2], (IMAGES, E), 0.125, 0.75, ((0, 128), (1, 8))),
        "head": gaussian(seeds[3], (D, E), E ** -0.5, 0.078125, ((1, 8),)),
        "sample_id": with_ends(jax.random.randint(seeds[4], (IMAGES,), 0, IMAGES // 4), jax.random.fold_in(seeds[4], 1), 0, (IMAGES // 4) - 1).astype(jnp.int32),
        "domain": with_ends(ranked_ids(seeds[5], (IMAGES,), DOMAINS, 2), jax.random.fold_in(seeds[5], 3), 0, DOMAINS - 1).astype(jnp.int32),
        "domain_bias": jnp.clip(jax.random.uniform(seeds[6], (DOMAINS,), jnp.float32, -6.0, -1.0), -6.0, -1.0),
    }


epsilon = 1e-06
similarity_scaling_factor = 10.0

def to_unit(values):
    floats = values.astype(jnp.float32)
    norms = jnp.sqrt(lax.optimization_barrier(jnp.sum(floats * floats, -1, keepdims=True)) + epsilon)
    return (floats / norms, norms)

def unit_back(unit_vals, norms, cotangent):
    return (cotangent - unit_vals * lax.optimization_barrier(jnp.sum(unit_vals * cotangent, -1, keepdims=True))) / norms

def reference(image_embed, text_embed, image_feat, head, sample_id, domain, domain_bias):
    image_unit, image_norm = to_unit(image_embed)
    text_unit, text_norm = to_unit(text_embed)
    image_round = image_unit.astype(jnp.bfloat16)
    text_round = text_unit.astype(jnp.bfloat16)
    table = jnp.arange(DOMAINS, dtype=jnp.int32)
    pair_bias = lax.optimization_barrier(jnp.sum(jnp.where(domain[:, None] == table[None, :], domain_bias[None, :], 0.0), -1))

    def slope_tile(image_block, text_block):
        image_start = (image_block * B_BLK).astype(jnp.int32)
        text_start = (text_block * B_BLK).astype(jnp.int32)
        picture_sample_range = lax.dynamic_slice_in_dim(image_round, image_start, B_BLK, 0)
        caption_sample_range = lax.dynamic_slice_in_dim(text_round, text_start, B_BLK, 0)
        image_ids = lax.dynamic_slice_in_dim(sample_id, image_start, B_BLK, 0)
        text_ids = lax.dynamic_slice_in_dim(sample_id, text_start, B_BLK, 0)
        caption_score_offset = lax.dynamic_slice_in_dim(pair_bias, text_start, B_BLK, 0)
        similarity_scores = similarity_scaling_factor * lax.dot_general(picture_sample_range, caption_sample_range, (((1,), (1,)), ((), ())), preferred_element_type=jnp.float32) + caption_score_offset[None, :]
        signs = jnp.where(image_ids[:, None] == text_ids[None, :], 1.0, -1.0).astype(jnp.float32)
        objective_derivative = (-signs * jax.nn.sigmoid(-signs * similarity_scores)).astype(jnp.bfloat16)
        return (objective_derivative, picture_sample_range, caption_sample_range)

    def image_side(image_block):
        objective_grand_sum = jnp.zeros((B_BLK, D), jnp.float32)
        for offset in range(STEPS):
            text_block = (image_block - offset) % N_BLK
            objective_derivative, picture_sample_range, caption_sample_range = slope_tile(image_block, text_block)
            objective_grand_sum = objective_grand_sum + similarity_scaling_factor * jnp.dot(objective_derivative, caption_sample_range, preferred_element_type=jnp.float32)
        return objective_grand_sum

    def text_side(text_block):
        objective_grand_sum = jnp.zeros((B_BLK, D), jnp.float32)
        for offset in range(STEPS):
            image_block = (text_block + offset) % N_BLK
            objective_derivative, picture_sample_range, caption_sample_range = slope_tile(image_block, text_block)
            objective_grand_sum = objective_grand_sum + similarity_scaling_factor * lax.dot_general(objective_derivative, picture_sample_range, (((0,), (0,)), ((), ())), preferred_element_type=jnp.float32)
        return objective_grand_sum
    blocks = jnp.arange(N_BLK, dtype=jnp.int32)
    picture_unit_vector = lax.map(image_side, blocks).reshape(IMAGES, D)
    text_dir = lax.map(text_side, blocks).reshape(IMAGES, D)
    embed_grad = unit_back(image_unit, image_norm, picture_unit_vector).astype(jnp.bfloat16)
    text_grad = unit_back(text_unit, text_norm, text_dir)
    image_grad = jnp.dot(embed_grad, head, preferred_element_type=jnp.float32).astype(jnp.bfloat16)
    head_grad = lax.dot_general(embed_grad, image_feat, (((0,), (0,)), ((), ())), preferred_element_type=jnp.float32)
    return (image_grad, text_grad, head_grad)
```

```python
import functools

import jax
import jax.numpy as jnp
from jax import lax
from jax.experimental import pallas as pl
from jax.experimental.pallas import tpu as pltpu
from jax.sharding import Mesh, PartitionSpec as P

EPSILON = 1e-06
SCALE = 10.0
TAIL = 128
SPLIT = (("xh", 2), ("z", 8), ("y", 8), ("xl", 4), ("core", 2))
BLK = ("xh", "z", "y")
TOWER = ("xl", "core")
ALL = BLK + TOWER

bf16, f32, i32 = jnp.bfloat16, jnp.float32, jnp.int32
NT = (((1,), (1,)), ((), ()))
TN = (((0,), (0,)), ((), ()))
PARAMS = pltpu.CompilerParams(vmem_limit_bytes=32 * 1024 * 1024)


def shifted(block, axis, distance):
    size = lax.axis_size(axis)
    return lax.ppermute(block, axis, [((i - distance) % size, i) for i in range(size)])


def norms_of(floats):
    return jnp.sqrt(jnp.sum(floats * floats, -1, keepdims=True) + EPSILON)


def vmem(count):
    return [pl.BlockSpec(memory_space=pltpu.VMEM)] * count


def iota(shape, dim):
    return lax.broadcasted_iota(i32, shape, dim)


def prepare(pos_ref, bias_ref, text_ref, ids_ref, domain_ref, out_ref):
    rows, width = text_ref.shape
    floats = text_ref[...].astype(f32)
    out_ref[:, :width] = (floats / norms_of(floats)).astype(bf16)
    wide = (rows, ids_ref.shape[1])
    mine = iota(wide, 1) == iota(wide, 0) + pos_ref[0] * rows
    own_id = jnp.sum(jnp.where(mine, ids_ref[...].astype(f32), 0.0), -1, keepdims=True)
    own_domain = jnp.sum(jnp.where(mine, domain_ref[...].astype(f32), 0.0), -1, keepdims=True)
    bias = jnp.zeros((rows, 1), f32)
    for k in range(bias_ref.shape[0]):
        bias = bias + jnp.where(own_domain == float(k), bias_ref[k], 0.0)
    whole = own_id.astype(i32)
    high = (whole >> 6).astype(f32)
    low = (whole & 63).astype(f32)
    first = bias.astype(bf16).astype(f32)
    second = (bias - first).astype(bf16).astype(f32)
    third = bias - first - second
    lane = iota((rows, TAIL), 1)
    tail = jnp.zeros((rows, TAIL), f32)
    for k, part in enumerate((high, low, first, second, third)):
        tail = jnp.where(lane == k, part, tail)
    out_ref[:, width:] = tail.astype(bf16)


def slopes(rows, image_round, ids):
    width = image_round.shape[1]
    images = image_round.shape[0]
    tail = rows[:, width:]
    which = iota((TAIL, images), 0)
    take_id = jnp.where(which == 0, 64.0, jnp.where(which == 1, 1.0, 0.0)).astype(bf16)
    take_bias = jnp.where((which >= 2) & (which < 5), 1.0, 0.0).astype(bf16)
    logits = SCALE * lax.dot_general(rows[:, :width], image_round, NT, preferred_element_type=f32)
    logits = logits + jnp.dot(tail, take_bias, preferred_element_type=f32)
    text_ids = jnp.dot(tail, take_id, preferred_element_type=f32)
    signs = jnp.where(text_ids == ids.astype(f32), 1.0, -1.0)
    return (-signs * jax.nn.sigmoid(-signs * logits)).astype(bf16)


def text_side(own_ref, image_ref, ids_ref, near_ref, far_ref):
    slope = slopes(own_ref[...], image_ref[...], ids_ref[...])
    share = SCALE * jnp.dot(slope, image_ref[...], preferred_element_type=f32)
    half = near_ref.shape[0]
    near_ref[...] = share[:half]
    far_ref[...] = share[half:].astype(far_ref.dtype)


def image_side(a_ref, b_ref, embed_ref, ids_ref, out_ref, turned_ref):
    floats = embed_ref[...].astype(f32)
    norms = norms_of(floats)
    units = floats / norms
    rounded = units.astype(bf16)
    width = floats.shape[1]
    total = jnp.zeros(floats.shape, f32)
    for ref in (a_ref, b_ref):
        rows = ref[...]
        slope = slopes(rows, rounded, ids_ref[...])
        total = total + lax.dot_general(slope, rows[:, :width], TN, preferred_element_type=f32)
    total = SCALE * total
    grad = (total - units * jnp.sum(units * total, -1, keepdims=True)) / norms
    out_ref[...] = grad.astype(bf16)
    turned = grad.T.astype(bf16)
    planes, pieces, run = turned_ref.shape[0], turned_ref.shape[1], turned_ref.shape[2]
    for p in range(pieces):
        for z in range(planes):
            start = (p * planes + z) * run
            turned_ref[z, p] = turned[start : start + run]


def head_side(turned_ref, feat_ref, out_ref):
    blocks = turned_ref.shape[0]
    part = jnp.zeros((turned_ref.shape[1], feat_ref.shape[2]), f32)
    for k in range(blocks):
        part = part + jnp.dot(turned_ref[k], feat_ref[k], preferred_element_type=f32)
    targets, groups = out_ref.shape[0], part.shape[1] // 128
    run = part.shape[0] // targets
    for c in range(targets):
        for g in range(groups):
            out_ref[c, g * run : (g + 1) * run] = part[
                c * run : (c + 1) * run, g * 128 : (g + 1) * 128
            ].astype(bf16)


def head_sum(parts_ref, out_ref):
    total = jnp.sum(parts_ref[...].astype(f32), 0)
    run, groups = out_ref.shape[0], out_ref.shape[1] // 128
    for g in range(groups):
        out_ref[:, g * 128 : (g + 1) * 128] = total[g * run : (g + 1) * run]


def text_back(share_ref, last_ref, text_ref, out_ref):
    floats = text_ref[...].astype(f32)
    norms = norms_of(floats)
    units = floats / norms
    total = share_ref[...] + last_ref[...].astype(f32)
    out_ref[...] = (total - units * jnp.sum(units * total, -1, keepdims=True)) / norms


def call(kernel, shapes, *args, smem=0):
    specs = [pl.BlockSpec(memory_space=pltpu.SMEM)] * smem + vmem(len(args) - smem)
    outs = [jax.ShapeDtypeStruct(s, d) for s, d in shapes]
    single = len(outs) == 1
    return pl.pallas_call(
        kernel,
        out_shape=outs[0] if single else outs,
        in_specs=specs,
        out_specs=vmem(1)[0] if single else vmem(len(outs)),
        compiler_params=PARAMS,
        name=kernel.__name__,
    )(*args)


def local(image_embed, text_embed, image_feat, head, sample_id, domain, domain_bias):
    images, width = image_embed.shape
    texts = text_embed.shape[0]
    features = image_feat.shape[1]
    position = lax.axis_index(TOWER).astype(i32).reshape(1)
    ids = sample_id.reshape(1, images)
    planes = lax.axis_size("z")
    across = lax.axis_size("xh") * lax.axis_size("y")
    own_width = width // planes

    feats = lax.all_gather(image_feat, "z", axis=0, tiled=False)

    payload = call(
        prepare, [((texts, width + TAIL), bf16)],
        position, domain_bias, text_embed, ids, domain.reshape(1, images), smem=2,
    )
    floats = image_embed.astype(f32)
    image_round = (floats / norms_of(floats)).astype(bf16)

    two = jnp.concatenate([payload, shifted(payload, BLK, 1)], 0)
    own = jnp.concatenate([two, shifted(two, BLK, 2)], 0)

    turns = [shifted(own, "xl", d) for d in range(1, lax.axis_size("xl"))]
    near, far = call(
        text_side, [((2 * texts, width), f32), ((2 * texts, width), bf16)],
        own, image_round, ids,
    )
    here = jnp.concatenate([own] + turns, 0)
    there = shifted(here, "core", 1)

    back = shifted(far, BLK, -2).astype(f32)
    stay = near[:texts] + back[:texts]
    pass_on = (near[texts:] + back[texts:]).astype(bf16)
    last = shifted(pass_on, BLK, -1)
    text_grad = call(text_back, [((texts, width), f32)], stay, last, text_embed)

    pieces = lax.axis_size("xh")
    run = width // (planes * pieces)
    embed_grad, turned = call(
        image_side,
        [((images, width), bf16), ((planes, pieces, run, images), bf16)],
        here, there, image_embed, ids,
    )
    plane = lax.all_to_all(turned.reshape(planes, own_width, images), "z", 0, 0, tiled=True)
    image_grad = jnp.dot(embed_grad, head, preferred_element_type=f32).astype(bf16)
    rows = own_width // across
    parts = call(
        head_side, [((across, rows * features // 128, 128), bf16)], plane, feats
    )
    parts = lax.all_to_all(parts, ("xh", "y"), 0, 0, tiled=True)
    head_grad = call(head_sum, [((rows, features), f32)], parts)
    return (image_grad, text_grad, head_grad)


def solution(mesh):
    split = Mesh(mesh.devices.reshape([n for _, n in SPLIT]), [name for name, _ in SPLIT])
    in_specs = (
        P(BLK, None),
        P(ALL, None),
        P(BLK, TOWER),
        P(None, TOWER),
        P(BLK),
        P(BLK),
        P(),
    )
    out_specs = (P(BLK, TOWER), P(ALL, None), P(BLK, TOWER))
    return jax.shard_map(local, mesh=split, in_specs=in_specs, out_specs=out_specs, check_vma=False)
```

```python
import functools

import jax
import jax.numpy as jnp
from jax import lax
from jax.experimental import pallas as pl
from jax.experimental.pallas import tpu as pltpu
from jax.sharding import Mesh, PartitionSpec as P

EPSILON = 1e-06
SCALE = 10.0
TAIL = 128
SPLIT = (("xh", 2), ("z", 8), ("y", 8), ("xl", 4), ("core", 2))
BLK = ("xh", "z", "y")
TOWER = ("xl", "core")
ALL = BLK + TOWER

bf16, f32, i32 = jnp.bfloat16, jnp.float32, jnp.int32
NT = (((1,), (1,)), ((), ()))
TN = (((0,), (0,)), ((), ()))
PARAMS = pltpu.CompilerParams(vmem_limit_bytes=32 * 1024 * 1024)


def shifted(block, axis, distance):
    size = lax.axis_size(axis)
    return lax.ppermute(block, axis, [((i - distance) % size, i) for i in range(size)])


def norms_of(floats):
    return jnp.sqrt(jnp.sum(floats * floats, -1, keepdims=True) + EPSILON)


def vmem(count):
    return [pl.BlockSpec(memory_space=pltpu.VMEM)] * count


def iota(shape, dim):
    return lax.broadcasted_iota(i32, shape, dim)


def prepare(pos_ref, bias_ref, text_ref, ids_ref, domain_ref, out_ref):
    rows, width = text_ref.shape
    floats = text_ref[...].astype(f32)
    out_ref[:, :width] = (floats / norms_of(floats)).astype(bf16)
    wide = (rows, ids_ref.shape[1])
    mine = iota(wide, 1) == iota(wide, 0) + pos_ref[0] * rows
    own_id = jnp.sum(jnp.where(mine, ids_ref[...].astype(f32), 0.0), -1, keepdims=True)
    own_domain = jnp.sum(jnp.where(mine, domain_ref[...].astype(f32), 0.0), -1, keepdims=True)
    bias = jnp.zeros((rows, 1), f32)
    for k in range(bias_ref.shape[0]):
        bias = bias + jnp.where(own_domain == float(k), bias_ref[k], 0.0)
    whole = own_id.astype(i32)
    high = (whole >> 6).astype(f32)
    low = (whole & 63).astype(f32)
    first = bias.astype(bf16).astype(f32)
    second = (bias - first).astype(bf16).astype(f32)
    third = bias - first - second
    lane = iota((rows, TAIL), 1)
    tail = jnp.zeros((rows, TAIL), f32)
    for k, part in enumerate((high, low, first, second, third)):
        tail = jnp.where(lane == k, part, tail)
    out_ref[:, width:] = tail.astype(bf16)


def slopes(rows, image_round, ids):
    width = image_round.shape[1]
    images = image_round.shape[0]
    tail = rows[:, width:]
    which = iota((TAIL, images), 0)
    take_id = jnp.where(which == 0, 64.0, jnp.where(which == 1, 1.0, 0.0)).astype(bf16)
    take_bias = jnp.where((which >= 2) & (which < 5), 1.0, 0.0).astype(bf16)
    logits = SCALE * lax.dot_general(rows[:, :width], image_round, NT, preferred_element_type=f32)
    logits = logits + jnp.dot(tail, take_bias, preferred_element_type=f32)
    text_ids = jnp.dot(tail, take_id, preferred_element_type=f32)
    signs = jnp.where(text_ids == ids.astype(f32), 1.0, -1.0)
    return (-signs * jax.nn.sigmoid(-signs * logits)).astype(bf16)


def text_side(own_ref, image_ref, ids_ref, kept_ref, away_ref):
    slope = slopes(own_ref[...], image_ref[...], ids_ref[...])
    share = SCALE * jnp.dot(slope, image_ref[...], preferred_element_type=f32)
    count = kept_ref.shape[0]
    kept_ref[...] = share[:count]
    away_ref[...] = share[count:].astype(away_ref.dtype)


def image_side(a_ref, b_ref, embed_ref, ids_ref, _away, out_ref, turned_ref):
    floats = embed_ref[...].astype(f32)
    norms = norms_of(floats)
    units = floats / norms
    rounded = units.astype(bf16)
    width = floats.shape[1]
    total = jnp.zeros(floats.shape, f32)
    for ref in (a_ref, b_ref):
        rows = ref[...]
        slope = slopes(rows, rounded, ids_ref[...])
        total = total + lax.dot_general(slope, rows[:, :width], TN, preferred_element_type=f32)
    total = SCALE * total
    grad = (total - units * jnp.sum(units * total, -1, keepdims=True)) / norms
    out_ref[...] = grad.astype(bf16)
    turned = grad.T.astype(bf16)
    planes, pieces, run = turned_ref.shape[0], turned_ref.shape[1], turned_ref.shape[2]
    for p in range(pieces):
        for z in range(planes):
            start = (p * planes + z) * run
            turned_ref[z, p] = turned[start : start + run]


def head_side(turned_ref, feat_ref, out_ref):
    blocks = turned_ref.shape[0]
    part = jnp.zeros((turned_ref.shape[1], feat_ref.shape[2]), f32)
    for k in range(blocks):
        part = part + jnp.dot(turned_ref[k], feat_ref[k], preferred_element_type=f32)
    targets, groups = out_ref.shape[0], part.shape[1] // 128
    run = part.shape[0] // targets
    for c in range(targets):
        for g in range(groups):
            out_ref[c, g * run : (g + 1) * run] = part[
                c * run : (c + 1) * run, g * 128 : (g + 1) * 128
            ].astype(bf16)


def head_sum(parts_ref, out_ref):
    total = jnp.sum(parts_ref[...].astype(f32), 0)
    run, groups = out_ref.shape[0], out_ref.shape[1] // 128
    for g in range(groups):
        out_ref[:, g * 128 : (g + 1) * 128] = total[g * run : (g + 1) * run]


def text_back(share_ref, one_ref, two_ref, three_ref, text_ref, out_ref):
    floats = text_ref[...].astype(f32)
    norms = norms_of(floats)
    units = floats / norms
    total = share_ref[...]
    for ref in (one_ref, two_ref, three_ref):
        total = total + ref[...].astype(f32)
    out_ref[...] = (total - units * jnp.sum(units * total, -1, keepdims=True)) / norms


def call(kernel, shapes, *args, smem=0, after=0):
    specs = [pl.BlockSpec(memory_space=pltpu.SMEM)] * smem + vmem(len(args) - smem - after)
    specs += [pl.BlockSpec(memory_space=pl.ANY)] * after
    outs = [jax.ShapeDtypeStruct(s, d) for s, d in shapes]
    single = len(outs) == 1
    return pl.pallas_call(
        kernel,
        out_shape=outs[0] if single else outs,
        in_specs=specs,
        out_specs=vmem(1)[0] if single else vmem(len(outs)),
        compiler_params=PARAMS,
        name=kernel.__name__,
    )(*args)


def local(image_embed, text_embed, image_feat, head, sample_id, domain, domain_bias):
    images, width = image_embed.shape
    texts = text_embed.shape[0]
    features = image_feat.shape[1]
    position = lax.axis_index(TOWER).astype(i32).reshape(1)
    ids = sample_id.reshape(1, images)
    planes = lax.axis_size("z")
    across = lax.axis_size("xh") * lax.axis_size("y")
    own_width = width // planes

    payload = call(
        prepare, [((texts, width + TAIL), bf16)],
        position, domain_bias, text_embed, ids, domain.reshape(1, images), smem=2,
    )
    payload, feat = lax.optimization_barrier((payload, image_feat))
    feats = jnp.broadcast_to(feat[None], (planes, images, features))
    feats = lax.all_to_all(feats, "z", 0, 0, tiled=True)
    floats = image_embed.astype(f32)
    image_round = (floats / norms_of(floats)).astype(bf16)

    own = jnp.concatenate([payload] + [shifted(payload, BLK, d) for d in (1, 2, 3)], 0)

    turns = [shifted(own, "xl", d) for d in range(1, lax.axis_size("xl"))]
    kept, away = call(
        text_side, [((texts, width), f32), ((3 * texts, width), bf16)],
        own, image_round, ids,
    )
    here = jnp.concatenate([own] + turns, 0)
    there = shifted(here, "core", 1)

    pieces = lax.axis_size("xh")
    run = width // (planes * pieces)
    embed_grad, turned = call(
        image_side,
        [((images, width), bf16), ((planes, pieces, run, images), bf16)],
        here, there, image_embed, ids, away, after=1,
    )
    turned, feats = lax.optimization_barrier((turned, feats))
    plane = lax.all_to_all(turned.reshape(planes, own_width, images), "z", 0, 0, tiled=True)

    backs = [shifted(away[(d - 1) * texts : d * texts], BLK, -d) for d in (1, 2, 3)]

    rows = own_width // across
    parts = call(
        head_side, [((across, rows * features // 128, 128), bf16)], plane, feats
    )
    parts = lax.all_to_all(parts, ("xh", "y"), 0, 0, tiled=True)
    text_grad = call(text_back, [((texts, width), f32)], kept, *backs, text_embed)
    image_grad = jnp.dot(embed_grad, head, preferred_element_type=f32).astype(bf16)
    head_grad = call(head_sum, [((rows, features), f32)], parts)
    return (image_grad, text_grad, head_grad)


def solution(mesh):
    split = Mesh(mesh.devices.reshape([n for _, n in SPLIT]), [name for name, _ in SPLIT])
    in_specs = (
        P(BLK, None),
        P(ALL, None),
        P(BLK, TOWER),
        P(None, TOWER),
        P(BLK),
        P(BLK),
        P(),
    )
    out_specs = (P(BLK, TOWER), P(ALL, None), P(BLK, TOWER))
    return jax.shard_map(local, mesh=split, in_specs=in_specs, out_specs=out_specs, check_vma=False)
```

```python
import functools

import jax
import jax.numpy as jnp
from jax import lax
from jax.experimental import pallas as pl
from jax.experimental.pallas import tpu as pltpu
from jax.sharding import Mesh, PartitionSpec as P

EPSILON = 1e-06
SCALE = 10.0
TAIL = 128
SPLIT = (("xh", 2), ("z", 8), ("y", 8), ("xl", 4), ("core", 2))
BLK = ("xh", "z", "y")
TOWER = ("xl", "core")
ALL = BLK + TOWER

bf16, f32, i32 = jnp.bfloat16, jnp.float32, jnp.int32
NT = (((1,), (1,)), ((), ()))
TN = (((0,), (0,)), ((), ()))
ROOM = 32 * 1024 * 1024


def shifted(block, axis, distance):
    size = lax.axis_size(axis)
    return lax.ppermute(block, axis, [((i - distance) % size, i) for i in range(size)])


def norms_of(floats):
    return jnp.sqrt(jnp.sum(floats * floats, -1, keepdims=True) + EPSILON)


def vmem(count):
    return [pl.BlockSpec(memory_space=pltpu.VMEM)] * count


def iota(shape, dim):
    return lax.broadcasted_iota(i32, shape, dim)


def prepare(pos_ref, text_hbm, ids_hbm, domain_hbm, bias_hbm, out_ref, text_ref, ids_ref, domain_ref, bias_ref, sems):
    pairs = ((text_hbm, text_ref), (ids_hbm, ids_ref), (domain_hbm, domain_ref), (bias_hbm, bias_ref))
    copies = [pltpu.make_async_copy(src, dst, sems.at[k]) for k, (src, dst) in enumerate(pairs)]
    for copy in copies:
        copy.start()
    for copy in copies:
        copy.wait()
    rows, width = text_ref.shape
    floats = text_ref[...].astype(f32)
    out_ref[:, :width] = (floats / norms_of(floats)).astype(bf16)
    wide = (rows, ids_ref.shape[1])
    mine = iota(wide, 1) == iota(wide, 0) + pos_ref[0] * rows
    own_id = jnp.sum(jnp.where(mine, ids_ref[...].astype(f32), 0.0), -1, keepdims=True)
    own_domain = jnp.sum(jnp.where(mine, domain_ref[...].astype(f32), 0.0), -1, keepdims=True)
    table = (rows, bias_ref.shape[1])
    chosen = own_domain.astype(i32) == iota(table, 1)
    bias = jnp.sum(jnp.where(chosen, jnp.broadcast_to(bias_ref[...], table), 0.0), -1, keepdims=True)
    whole = own_id.astype(i32)
    high = (whole >> 6).astype(f32)
    low = (whole & 63).astype(f32)
    first = bias.astype(bf16).astype(f32)
    second = (bias - first).astype(bf16).astype(f32)
    third = bias - first - second
    lane = iota((rows, TAIL), 1)
    tail = jnp.zeros((rows, TAIL), f32)
    for k, part in enumerate((high, low, first, second, third)):
        tail = jnp.where(lane == k, part, tail)
    out_ref[:, width:] = tail.astype(bf16)


def fan_out(embed_ref, feat_ref, _payload, round_ref, feats_hbm, sem):
    copies = [pltpu.make_async_copy(feat_ref, feats_hbm.at[k], sem) for k in range(feats_hbm.shape[0])]
    for copy in copies:
        copy.start()
    floats = embed_ref[...].astype(f32)
    round_ref[...] = (floats / norms_of(floats)).astype(bf16)
    for copy in copies:
        copy.wait()


def slopes(rows, image_round, ids):
    width = image_round.shape[1]
    images = image_round.shape[0]
    tail = rows[:, width:]
    which = iota((TAIL, images), 0)
    take_id = jnp.where(which == 0, 64.0, jnp.where(which == 1, 1.0, 0.0)).astype(bf16)
    take_bias = jnp.where((which >= 2) & (which < 5), 1.0, 0.0).astype(bf16)
    logits = SCALE * lax.dot_general(rows[:, :width], image_round, NT, preferred_element_type=f32)
    logits = logits + jnp.dot(tail, take_bias, preferred_element_type=f32)
    text_ids = jnp.dot(tail, take_id, preferred_element_type=f32)
    signs = jnp.where(text_ids == ids.astype(f32), 1.0, -1.0)
    return (-signs * jax.nn.sigmoid(-signs * logits)).astype(bf16)


def text_side(own_ref, image_ref, ids_ref, kept_ref, one_ref, two_ref, three_ref):
    slope = slopes(own_ref[...], image_ref[...], ids_ref[...])
    share = SCALE * jnp.dot(slope, image_ref[...], preferred_element_type=f32)
    count = kept_ref.shape[0]
    for k, ref in enumerate((kept_ref, one_ref, two_ref, three_ref)):
        ref[...] = share[k * count : (k + 1) * count].astype(ref.dtype)


def image_side(a_ref, b_ref, embed_ref, ids_ref, out_ref, turned_ref):
    floats = embed_ref[...].astype(f32)
    norms = norms_of(floats)
    units = floats / norms
    rounded = units.astype(bf16)
    width = floats.shape[1]
    total = jnp.zeros(floats.shape, f32)
    for ref in (a_ref, b_ref):
        rows = ref[...]
        slope = slopes(rows, rounded, ids_ref[...])
        total = total + lax.dot_general(slope, rows[:, :width], TN, preferred_element_type=f32)
    total = SCALE * total
    grad = (total - units * jnp.sum(units * total, -1, keepdims=True)) / norms
    out_ref[...] = grad.astype(bf16)
    turned = grad.T.astype(bf16)
    planes, pieces, run = turned_ref.shape[0], turned_ref.shape[1], turned_ref.shape[2]
    for p in range(pieces):
        for z in range(planes):
            start = (p * planes + z) * run
            turned_ref[z, p] = turned[start : start + run]


def head_side(turned_ref, feat_ref, out_ref):
    blocks = turned_ref.shape[0]
    part = jnp.zeros((turned_ref.shape[1], feat_ref.shape[2]), f32)
    for k in range(blocks):
        part = part + jnp.dot(turned_ref[k], feat_ref[k], preferred_element_type=f32)
    targets, groups = out_ref.shape[0], part.shape[1] // 128
    run = part.shape[0] // targets
    for c in range(targets):
        for g in range(groups):
            out_ref[c, g * run : (g + 1) * run] = part[
                c * run : (c + 1) * run, g * 128 : (g + 1) * 128
            ].astype(bf16)


def head_sum(parts_ref, out_ref):
    total = jnp.sum(parts_ref[...].astype(f32), 0)
    run, groups = out_ref.shape[0], out_ref.shape[1] // 128
    for g in range(groups):
        out_ref[:, g * 128 : (g + 1) * 128] = total[g * run : (g + 1) * run]


def text_back(share_ref, one_ref, two_ref, three_ref, text_ref, out_ref):
    floats = text_ref[...].astype(f32)
    norms = norms_of(floats)
    units = floats / norms
    total = share_ref[...]
    for ref in (one_ref, two_ref, three_ref):
        total = total + ref[...].astype(f32)
    out_ref[...] = (total - units * jnp.sum(units * total, -1, keepdims=True)) / norms


def call(kernel, shapes, *args, smem=0, hbm=0, after=0, out_hbm=0, scratch=(), cost=None, room=None):
    specs = [pl.BlockSpec(memory_space=pltpu.SMEM)] * smem
    specs += [pl.BlockSpec(memory_space=pltpu.HBM)] * hbm
    specs += vmem(len(args) - smem - hbm - after)
    specs += [pl.BlockSpec(memory_space=pl.ANY)] * after
    outs = [jax.ShapeDtypeStruct(s, d) for s, d in shapes]
    out_specs = vmem(len(outs) - out_hbm) + [pl.BlockSpec(memory_space=pltpu.HBM)] * out_hbm
    single = len(outs) == 1
    return pl.pallas_call(
        kernel,
        out_shape=outs[0] if single else outs,
        in_specs=specs,
        out_specs=out_specs[0] if single else out_specs,
        scratch_shapes=list(scratch),
        compiler_params=pltpu.CompilerParams(vmem_limit_bytes=room),
        cost_estimate=cost,
        name=kernel.__name__,
    )(*args)


def lasting(us):
    return pl.CostEstimate(flops=int(us * 1e9), bytes_accessed=0, transcendentals=0)


def local(image_embed, text_embed, image_feat, head, sample_id, domain, domain_bias):
    images, width = image_embed.shape
    texts = text_embed.shape[0]
    features = image_feat.shape[1]
    position = lax.axis_index(TOWER).astype(i32).reshape(1)
    ids = sample_id.reshape(1, images)
    planes = lax.axis_size("z")
    across = lax.axis_size("xh") * lax.axis_size("y")
    own_width = width // planes

    inputs = (text_embed, ids, domain.reshape(1, images), domain_bias.reshape(1, -1))
    payload = call(
        prepare, [((texts, width + TAIL), bf16)], position, *inputs, smem=1, hbm=4,
        scratch=[pltpu.VMEM(v.shape, v.dtype) for v in inputs] + [pltpu.SemaphoreType.DMA((4,))],
    )
    image_round, feats = call(
        fan_out, [((images, width), bf16), ((planes, images, features), bf16)],
        image_embed, image_feat, payload, after=1, out_hbm=1,
        scratch=[pltpu.SemaphoreType.DMA], cost=lasting(20),
    )
    feats = lax.all_to_all(feats, "z", 0, 0, tiled=True)

    own = jnp.concatenate([payload] + [shifted(payload, BLK, d) for d in (1, 2, 3)], 0)

    here = lax.all_gather(own, "xl", axis=0, tiled=True)
    there = shifted(here, "core", 1)
    kept, *aways = call(
        text_side, [((texts, width), f32)] + [((texts, width), bf16)] * 3,
        own, image_round, ids,
    )

    pieces = lax.axis_size("xh")
    run = width // (planes * pieces)
    embed_grad, turned = call(
        image_side,
        [((images, width), bf16), ((planes, pieces, run, images), bf16)],
        here, there, image_embed, ids,
    )
    turned, feats = lax.optimization_barrier((turned, feats))
    plane = lax.all_to_all(turned.reshape(planes, own_width, images), "z", 0, 0, tiled=True)

    backs = [shifted(away, BLK, -d) for d, away in zip((1, 2, 3), aways)]

    rows = own_width // across
    parts = call(
        head_side, [((across, rows * features // 128, 128), bf16)], plane, feats, room=ROOM
    )
    parts = lax.all_to_all(parts, ("xh", "y"), 0, 0, tiled=True)
    text_grad = call(
        text_back, [((texts, width), f32)], kept, *backs, text_embed, cost=lasting(60), room=ROOM
    )
    image_grad = jnp.dot(embed_grad, head, preferred_element_type=f32).astype(bf16)
    head_grad = call(head_sum, [((rows, features), f32)], parts, room=ROOM)
    return (image_grad, text_grad, head_grad)


def solution(mesh):
    split = Mesh(mesh.devices.reshape([n for _, n in SPLIT]), [name for name, _ in SPLIT])
    in_specs = (
        P(BLK, None),
        P(ALL, None),
        P(BLK, TOWER),
        P(None, TOWER),
        P(BLK),
        P(BLK),
        P(),
    )
    out_specs = (P(BLK, TOWER), P(ALL, None), P(BLK, TOWER))
    return jax.shard_map(local, mesh=split, in_specs=in_specs, out_specs=out_specs, check_vma=False)
```

```python
import functools

import jax
import jax.numpy as jnp
from jax import lax
from jax.experimental import pallas as pl
from jax.experimental.pallas import tpu as pltpu
from jax.sharding import Mesh, PartitionSpec as P

EPSILON = 1e-06
SCALE = 10.0
TAIL = 128
SPLIT = (("xh", 2), ("z", 8), ("y", 8), ("xl", 4), ("core", 2))
BLK = ("xh", "z", "y")
TOWER = ("xl", "core")
ALL = BLK + TOWER

bf16, f32, i32 = jnp.bfloat16, jnp.float32, jnp.int32
NT = (((1,), (1,)), ((), ()))
TN = (((0,), (0,)), ((), ()))
ROOM = 32 * 1024 * 1024


def shifted(block, axis, distance):
    size = lax.axis_size(axis)
    return lax.ppermute(block, axis, [((i - distance) % size, i) for i in range(size)])


def norms_of(floats):
    return jnp.sqrt(jnp.sum(floats * floats, -1, keepdims=True) + EPSILON)


def vmem(count):
    return [pl.BlockSpec(memory_space=pltpu.VMEM)] * count


def iota(shape, dim):
    return lax.broadcasted_iota(i32, shape, dim)


def prepare(pos_ref, text_hbm, ids_hbm, domain_hbm, bias_hbm, out_ref, text_ref, ids_ref, domain_ref, bias_ref, sems):
    pairs = ((text_hbm, text_ref), (ids_hbm, ids_ref), (domain_hbm, domain_ref), (bias_hbm, bias_ref))
    copies = [pltpu.make_async_copy(src, dst, sems.at[k]) for k, (src, dst) in enumerate(pairs)]
    for copy in copies:
        copy.start()
    for copy in copies:
        copy.wait()
    rows, width = text_ref.shape
    floats = text_ref[...].astype(f32)
    out_ref[:, :width] = (floats / norms_of(floats)).astype(bf16)
    wide = (rows, ids_ref.shape[1])
    mine = iota(wide, 1) == iota(wide, 0) + pos_ref[0] * rows
    own_id = jnp.sum(jnp.where(mine, ids_ref[...].astype(f32), 0.0), -1, keepdims=True)
    own_domain = jnp.sum(jnp.where(mine, domain_ref[...].astype(f32), 0.0), -1, keepdims=True)
    table = (rows, bias_ref.shape[1])
    chosen = own_domain.astype(i32) == iota(table, 1)
    bias = jnp.sum(jnp.where(chosen, jnp.broadcast_to(bias_ref[...], table), 0.0), -1, keepdims=True)
    whole = own_id.astype(i32)
    high = (whole >> 6).astype(f32)
    low = (whole & 63).astype(f32)
    first = bias.astype(bf16).astype(f32)
    second = (bias - first).astype(bf16).astype(f32)
    third = bias - first - second
    lane = iota((rows, TAIL), 1)
    tail = jnp.zeros((rows, TAIL), f32)
    for k, part in enumerate((high, low, first, second, third)):
        tail = jnp.where(lane == k, part, tail)
    out_ref[:, width:] = tail.astype(bf16)


def fan_out(feat_hbm, _payload, feats_hbm, sem):
    copies = [pltpu.make_async_copy(feat_hbm, feats_hbm.at[k], sem) for k in range(feats_hbm.shape[0])]
    for copy in copies:
        copy.start()
    for copy in copies:
        copy.wait()


def assemble(*refs):
    out_ref, count = refs[-1], refs[0].shape[0]
    for k, ref in enumerate(refs[:-1]):
        out_ref[k * count : (k + 1) * count] = ref[...]


def slopes(rows, image_round, ids):
    width = image_round.shape[1]
    images = image_round.shape[0]
    tail = rows[:, width:]
    which = iota((TAIL, images), 0)
    take_id = jnp.where(which == 0, 64.0, jnp.where(which == 1, 1.0, 0.0)).astype(bf16)
    take_bias = jnp.where((which >= 2) & (which < 5), 1.0, 0.0).astype(bf16)
    logits = SCALE * lax.dot_general(rows[:, :width], image_round, NT, preferred_element_type=f32)
    logits = logits + jnp.dot(tail, take_bias, preferred_element_type=f32)
    text_ids = jnp.dot(tail, take_id, preferred_element_type=f32)
    signs = jnp.where(text_ids == ids.astype(f32), 1.0, -1.0)
    return (-signs * jax.nn.sigmoid(-signs * logits)).astype(bf16)


def text_shares(places, own_ref, embed_ref, ids_ref, refs):
    count = refs[0].shape[0]
    floats = embed_ref[...].astype(f32)
    rounded = (floats / norms_of(floats)).astype(bf16)
    rows = jnp.concatenate([own_ref[p * count : (p + 1) * count] for p in places], 0)
    slope = slopes(rows, rounded, ids_ref[...])
    share = SCALE * jnp.dot(slope, rounded, preferred_element_type=f32)
    for k, ref in enumerate(refs):
        ref[...] = share[k * count : (k + 1) * count].astype(ref.dtype)


def text_first(own_ref, embed_ref, ids_ref, _turned, one_ref, two_ref):
    text_shares((1, 2), own_ref, embed_ref, ids_ref, (one_ref, two_ref))


def text_second(own_ref, embed_ref, ids_ref, _parts, kept_ref, three_ref):
    text_shares((0, 3), own_ref, embed_ref, ids_ref, (kept_ref, three_ref))


def image_side(a_ref, b_ref, embed_ref, ids_ref, out_ref, turned_ref):
    floats = embed_ref[...].astype(f32)
    norms = norms_of(floats)
    units = floats / norms
    rounded = units.astype(bf16)
    width = floats.shape[1]
    total = jnp.zeros(floats.shape, f32)
    for ref in (a_ref, b_ref):
        rows = ref[...]
        slope = slopes(rows, rounded, ids_ref[...])
        total = total + lax.dot_general(slope, rows[:, :width], TN, preferred_element_type=f32)
    total = SCALE * total
    grad = (total - units * jnp.sum(units * total, -1, keepdims=True)) / norms
    out_ref[...] = grad.astype(bf16)
    turned = grad.T.astype(bf16)
    planes, pieces, run = turned_ref.shape[0], turned_ref.shape[1], turned_ref.shape[2]
    for p in range(pieces):
        for z in range(planes):
            start = (p * planes + z) * run
            turned_ref[z, p] = turned[start : start + run]


def head_side(turned_ref, feat_ref, _one, _two, out_ref):
    blocks = turned_ref.shape[0]
    part = jnp.zeros((turned_ref.shape[1], feat_ref.shape[2]), f32)
    for k in range(blocks):
        part = part + jnp.dot(turned_ref[k], feat_ref[k], preferred_element_type=f32)
    targets, groups = out_ref.shape[0], part.shape[1] // 128
    run = part.shape[0] // targets
    for c in range(targets):
        for g in range(groups):
            out_ref[c, g * run : (g + 1) * run] = part[
                c * run : (c + 1) * run, g * 128 : (g + 1) * 128
            ].astype(bf16)


def head_sum(parts_ref, out_ref):
    total = jnp.sum(parts_ref[...].astype(f32), 0)
    run, groups = out_ref.shape[0], out_ref.shape[1] // 128
    for g in range(groups):
        out_ref[:, g * 128 : (g + 1) * 128] = total[g * run : (g + 1) * run]


def text_back(share_ref, one_ref, two_ref, three_ref, text_ref, out_ref):
    floats = text_ref[...].astype(f32)
    norms = norms_of(floats)
    units = floats / norms
    total = share_ref[...]
    for ref in (one_ref, two_ref, three_ref):
        total = total + ref[...].astype(f32)
    out_ref[...] = (total - units * jnp.sum(units * total, -1, keepdims=True)) / norms


def call(kernel, shapes, *args, smem=0, hbm=0, after=0, out_hbm=0, scratch=(), cost=None, room=None):
    specs = [pl.BlockSpec(memory_space=pltpu.SMEM)] * smem
    specs += [pl.BlockSpec(memory_space=pltpu.HBM)] * hbm
    specs += vmem(len(args) - smem - hbm - after)
    specs += [pl.BlockSpec(memory_space=pl.ANY)] * after
    outs = [jax.ShapeDtypeStruct(s, d) for s, d in shapes]
    out_specs = vmem(len(outs) - out_hbm) + [pl.BlockSpec(memory_space=pltpu.HBM)] * out_hbm
    single = len(outs) == 1
    return pl.pallas_call(
        kernel,
        out_shape=outs[0] if single else outs,
        in_specs=specs,
        out_specs=out_specs[0] if single else out_specs,
        scratch_shapes=list(scratch),
        compiler_params=pltpu.CompilerParams(vmem_limit_bytes=room),
        cost_estimate=cost,
        name=kernel.__name__,
    )(*args)


def lasting(us):
    return pl.CostEstimate(flops=int(us * 1e9), bytes_accessed=0, transcendentals=0)


def local(image_embed, text_embed, image_feat, head, sample_id, domain, domain_bias):
    images, width = image_embed.shape
    texts = text_embed.shape[0]
    features = image_feat.shape[1]
    position = lax.axis_index(TOWER).astype(i32).reshape(1)
    ids = sample_id.reshape(1, images)
    planes = lax.axis_size("z")
    across = lax.axis_size("xh") * lax.axis_size("y")
    own_width = width // planes

    inputs = (text_embed, ids, domain.reshape(1, images), domain_bias.reshape(1, -1))
    payload = call(
        prepare, [((texts, width + TAIL), bf16)], position, *inputs, smem=1, hbm=4,
        scratch=[pltpu.VMEM(v.shape, v.dtype) for v in inputs] + [pltpu.SemaphoreType.DMA((4,))],
    )
    feats = call(
        fan_out, [((planes, images, features), bf16)], image_feat, payload,
        hbm=1, after=1, out_hbm=1, scratch=[pltpu.SemaphoreType.DMA], cost=lasting(20),
    )
    feats = lax.all_to_all(feats, "z", 0, 0, tiled=True)

    window = [payload] + [shifted(payload, BLK, d) for d in (1, 2, 3)]
    own = call(
        assemble, [((len(window) * texts, width + TAIL), bf16)], *window,
        cost=lasting(400), room=ROOM,
    )

    here = lax.all_gather(own, "xl", axis=0, tiled=True)
    there = shifted(here, "core", 1)

    pieces = lax.axis_size("xh")
    run = width // (planes * pieces)
    embed_grad, turned = call(
        image_side,
        [((images, width), bf16), ((planes, pieces, run, images), bf16)],
        here, there, image_embed, ids, room=ROOM,
    )
    shares = call(
        text_first, [((texts, width), bf16)] * 2, own, image_embed, ids, turned, after=1,
    )
    backs = [shifted(away, BLK, -d) for d, away in zip((1, 2), shares)]
    turned, feats = lax.optimization_barrier((turned, feats))
    plane = lax.all_to_all(turned.reshape(planes, own_width, images), "z", 0, 0, tiled=True)

    rows = own_width // across
    parts = call(
        head_side, [((across, rows * features // 128, 128), bf16)], plane, feats, *backs,
        after=2, room=ROOM,
    )
    kept, away = call(
        text_second, [((texts, width), f32), ((texts, width), bf16)],
        own, image_embed, ids, parts, after=1,
    )
    backs.append(shifted(away, BLK, -3))
    parts = lax.all_to_all(parts, ("xh", "y"), 0, 0, tiled=True)
    text_grad = call(
        text_back, [((texts, width), f32)], kept, *backs, text_embed, cost=lasting(1), room=ROOM
    )
    image_grad = jnp.dot(embed_grad, head, preferred_element_type=f32).astype(bf16)
    head_grad = call(head_sum, [((rows, features), f32)], parts, room=ROOM)
    return (image_grad, text_grad, head_grad)


def solution(mesh):
    split = Mesh(mesh.devices.reshape([n for _, n in SPLIT]), [name for name, _ in SPLIT])
    in_specs = (
        P(BLK, None),
        P(ALL, None),
        P(BLK, TOWER),
        P(None, TOWER),
        P(BLK),
        P(BLK),
        P(),
    )
    out_specs = (P(BLK, TOWER), P(ALL, None), P(BLK, TOWER))
    return jax.shard_map(local, mesh=split, in_specs=in_specs, out_specs=out_specs, check_vma=False)
```

```python
import functools

import jax
import jax.numpy as jnp
from jax import lax
from jax.experimental import pallas as pl
from jax.experimental.pallas import tpu as pltpu
from jax.sharding import Mesh, PartitionSpec as P

EPSILON = 1e-06
SCALE = 10.0
TAIL = 128
SPLIT = (("xh", 2), ("z", 8), ("y", 8), ("xl", 4), ("core", 2))
BLK = ("xh", "z", "y")
TOWER = ("xl", "core")
ALL = BLK + TOWER

bf16, f32, i32 = jnp.bfloat16, jnp.float32, jnp.int32
NT = (((1,), (1,)), ((), ()))
TN = (((0,), (0,)), ((), ()))
ROOM = 32 * 1024 * 1024


def shifted(block, axis, distance):
    size = lax.axis_size(axis)
    return lax.ppermute(block, axis, [((i - distance) % size, i) for i in range(size)])


def norms_of(floats):
    return jnp.sqrt(jnp.sum(floats * floats, -1, keepdims=True) + EPSILON)


def vmem(count):
    return [pl.BlockSpec(memory_space=pltpu.VMEM)] * count


def iota(shape, dim):
    return lax.broadcasted_iota(i32, shape, dim)


def prepare(pos_ref, text_hbm, ids_hbm, domain_hbm, bias_hbm, out_ref, text_ref, ids_ref, domain_ref, bias_ref, sems):
    pairs = ((text_hbm, text_ref), (ids_hbm, ids_ref), (domain_hbm, domain_ref), (bias_hbm, bias_ref))
    copies = [pltpu.make_async_copy(src, dst, sems.at[k]) for k, (src, dst) in enumerate(pairs)]
    for copy in copies:
        copy.start()
    for copy in copies:
        copy.wait()
    rows, width = text_ref.shape
    floats = text_ref[...].astype(f32)
    out_ref[:, :width] = (floats / norms_of(floats)).astype(bf16)
    wide = (rows, ids_ref.shape[1])
    mine = iota(wide, 1) == iota(wide, 0) + pos_ref[0] * rows
    own_id = jnp.sum(jnp.where(mine, ids_ref[...].astype(f32), 0.0), -1, keepdims=True)
    own_domain = jnp.sum(jnp.where(mine, domain_ref[...].astype(f32), 0.0), -1, keepdims=True)
    table = (rows, bias_ref.shape[1])
    chosen = own_domain.astype(i32) == iota(table, 1)
    bias = jnp.sum(jnp.where(chosen, jnp.broadcast_to(bias_ref[...], table), 0.0), -1, keepdims=True)
    whole = own_id.astype(i32)
    high = (whole >> 6).astype(f32)
    low = (whole & 63).astype(f32)
    first = bias.astype(bf16).astype(f32)
    second = (bias - first).astype(bf16).astype(f32)
    third = bias - first - second
    lane = iota((rows, TAIL), 1)
    tail = jnp.zeros((rows, TAIL), f32)
    for k, part in enumerate((high, low, first, second, third)):
        tail = jnp.where(lane == k, part, tail)
    out_ref[:, width:] = tail.astype(bf16)


def fan_out(feat_ref, _payload, feats_hbm, sem):
    copies = [pltpu.make_async_copy(feat_ref, feats_hbm.at[k], sem) for k in range(feats_hbm.shape[0])]
    for copy in copies:
        copy.start()
    for copy in copies:
        copy.wait()


def assemble(*refs):
    out_ref, count = refs[-1], refs[0].shape[0]
    for k, ref in enumerate(refs[:-1]):
        out_ref[k * count : (k + 1) * count] = ref[...]


def slopes(rows, image_round, ids):
    width = image_round.shape[1]
    images = image_round.shape[0]
    tail = rows[:, width:]
    which = iota((TAIL, images), 0)
    take_id = jnp.where(which == 0, 64.0, jnp.where(which == 1, 1.0, 0.0)).astype(bf16)
    take_bias = jnp.where((which >= 2) & (which < 5), 1.0, 0.0).astype(bf16)
    logits = SCALE * lax.dot_general(rows[:, :width], image_round, NT, preferred_element_type=f32)
    logits = logits + jnp.dot(tail, take_bias, preferred_element_type=f32)
    text_ids = jnp.dot(tail, take_id, preferred_element_type=f32)
    signs = jnp.where(text_ids == ids.astype(f32), 1.0, -1.0)
    return (-signs * jax.nn.sigmoid(-signs * logits)).astype(bf16)


def text_side(own_ref, embed_ref, ids_ref, _turned, *refs):
    floats = embed_ref[...].astype(f32)
    rounded = (floats / norms_of(floats)).astype(bf16)
    slope = slopes(own_ref[...], rounded, ids_ref[...])
    share = SCALE * jnp.dot(slope, rounded, preferred_element_type=f32)
    count = refs[0].shape[0]
    for k, ref in enumerate(refs):
        ref[...] = share[k * count : (k + 1) * count].astype(ref.dtype)


def image_side(a_ref, b_ref, embed_ref, ids_ref, out_ref, turned_ref):
    floats = embed_ref[...].astype(f32)
    norms = norms_of(floats)
    units = floats / norms
    rounded = units.astype(bf16)
    width = floats.shape[1]
    total = jnp.zeros(floats.shape, f32)
    for ref in (a_ref, b_ref):
        rows = ref[...]
        slope = slopes(rows, rounded, ids_ref[...])
        total = total + lax.dot_general(slope, rows[:, :width], TN, preferred_element_type=f32)
    total = SCALE * total
    grad = (total - units * jnp.sum(units * total, -1, keepdims=True)) / norms
    out_ref[...] = grad.astype(bf16)
    turned = grad.T.astype(bf16)
    planes, pieces, run = turned_ref.shape[0], turned_ref.shape[1], turned_ref.shape[2]
    for p in range(pieces):
        for z in range(planes):
            start = (p * planes + z) * run
            turned_ref[z, p] = turned[start : start + run]


def head_side(turned_ref, feat_ref, out_ref):
    blocks = turned_ref.shape[0]
    part = jnp.zeros((turned_ref.shape[1], feat_ref.shape[2]), f32)
    for k in range(blocks):
        part = part + jnp.dot(turned_ref[k], feat_ref[k], preferred_element_type=f32)
    targets, groups = out_ref.shape[0], part.shape[1] // 128
    run = part.shape[0] // targets
    for c in range(targets):
        for g in range(groups):
            out_ref[c, g * run : (g + 1) * run] = part[
                c * run : (c + 1) * run, g * 128 : (g + 1) * 128
            ].astype(bf16)


def head_sum(parts_ref, out_ref):
    total = jnp.sum(parts_ref[...].astype(f32), 0)
    run, groups = out_ref.shape[0], out_ref.shape[1] // 128
    for g in range(groups):
        out_ref[:, g * 128 : (g + 1) * 128] = total[g * run : (g + 1) * run]


def finish(grad_ref, head_ref, share_ref, one_ref, two_ref, three_ref, text_ref, image_ref, out_ref):
    image_ref[...] = jnp.dot(grad_ref[...], head_ref[...], preferred_element_type=f32).astype(bf16)
    floats = text_ref[...].astype(f32)
    norms = norms_of(floats)
    units = floats / norms
    total = share_ref[...]
    for ref in (one_ref, two_ref, three_ref):
        total = total + ref[...].astype(f32)
    out_ref[...] = (total - units * jnp.sum(units * total, -1, keepdims=True)) / norms


def call(kernel, shapes, *args, smem=0, hbm=0, after=0, out_hbm=0, scratch=(), cost=None, room=None):
    specs = [pl.BlockSpec(memory_space=pltpu.SMEM)] * smem
    specs += [pl.BlockSpec(memory_space=pltpu.HBM)] * hbm
    specs += vmem(len(args) - smem - hbm - after)
    specs += [pl.BlockSpec(memory_space=pl.ANY)] * after
    outs = [jax.ShapeDtypeStruct(s, d) for s, d in shapes]
    out_specs = vmem(len(outs) - out_hbm) + [pl.BlockSpec(memory_space=pltpu.HBM)] * out_hbm
    single = len(outs) == 1
    return pl.pallas_call(
        kernel,
        out_shape=outs[0] if single else outs,
        in_specs=specs,
        out_specs=out_specs[0] if single else out_specs,
        scratch_shapes=list(scratch),
        compiler_params=pltpu.CompilerParams(vmem_limit_bytes=room),
        cost_estimate=cost,
        name=kernel.__name__,
    )(*args)


def lasting(us):
    return pl.CostEstimate(flops=int(us * 1e9), bytes_accessed=0, transcendentals=0)


def local(image_embed, text_embed, image_feat, head, sample_id, domain, domain_bias):
    images, width = image_embed.shape
    texts = text_embed.shape[0]
    features = image_feat.shape[1]
    position = lax.axis_index(TOWER).astype(i32).reshape(1)
    ids = sample_id.reshape(1, images)
    planes = lax.axis_size("z")
    across = lax.axis_size("xh") * lax.axis_size("y")
    own_width = width // planes

    inputs = (text_embed, ids, domain.reshape(1, images), domain_bias.reshape(1, -1))
    payload = call(
        prepare, [((texts, width + TAIL), bf16)], position, *inputs, smem=1, hbm=4,
        scratch=[pltpu.VMEM(v.shape, v.dtype) for v in inputs] + [pltpu.SemaphoreType.DMA((4,))],
    )
    feats = call(
        fan_out, [((planes, images, features), bf16)], image_feat, payload,
        after=1, out_hbm=1, scratch=[pltpu.SemaphoreType.DMA], cost=lasting(20),
    )
    feats = lax.all_to_all(feats, "z", 0, 0, tiled=True)

    window = [payload] + [shifted(payload, BLK, d) for d in (1, 2, 3)]
    own = call(
        assemble, [((len(window) * texts, width + TAIL), bf16)], *window,
        cost=lasting(400), room=ROOM,
    )

    here = lax.all_gather(own, "xl", axis=0, tiled=True)
    there = shifted(here, "core", 1)

    pieces = lax.axis_size("xh")
    run = width // (planes * pieces)
    embed_grad, turned = call(
        image_side,
        [((images, width), bf16), ((planes, pieces, run, images), bf16)],
        here, there, image_embed, ids, room=ROOM,
    )
    turned, feats = lax.optimization_barrier((turned, feats))
    plane = lax.all_to_all(turned.reshape(planes, own_width, images), "z", 0, 0, tiled=True)

    kept, *aways = call(
        text_side, [((texts, width), f32)] + [((texts, width), bf16)] * 3,
        own, image_embed, ids, turned, after=1,
    )
    backs = [shifted(away, BLK, -d) for d, away in zip((1, 2, 3), aways)]

    rows = own_width // across
    parts = call(
        head_side, [((across, rows * features // 128, 128), bf16)], plane, feats, room=ROOM
    )
    parts = lax.all_to_all(parts, ("xh", "y"), 0, 0, tiled=True)
    image_grad, text_grad = call(
        finish, [((images, features), bf16), ((texts, width), f32)],
        embed_grad, head, kept, *backs, text_embed, cost=lasting(60), room=ROOM,
    )
    head_grad = call(head_sum, [((rows, features), f32)], parts, room=ROOM)
    return (image_grad, text_grad, head_grad)


def solution(mesh):
    split = Mesh(mesh.devices.reshape([n for _, n in SPLIT]), [name for name, _ in SPLIT])
    in_specs = (
        P(BLK, None),
        P(ALL, None),
        P(BLK, TOWER),
        P(None, TOWER),
        P(BLK),
        P(BLK),
        P(),
    )
    out_specs = (P(BLK, TOWER), P(ALL, None), P(BLK, TOWER))
    return jax.shard_map(local, mesh=split, in_specs=in_specs, out_specs=out_specs, check_vma=False)
```

```python
import functools

import jax
import jax.numpy as jnp
from jax import lax
from jax.experimental import pallas as pl
from jax.experimental.pallas import tpu as pltpu
from jax.sharding import Mesh, PartitionSpec as P

EPSILON = 1e-06
SCALE = 10.0
TAIL = 128
SPLIT = (("xh", 2), ("z", 8), ("y", 8), ("xl", 4), ("core", 2))
BLK = ("xh", "z", "y")
TOWER = ("xl", "core")
ALL = BLK + TOWER

bf16, f32, i32 = jnp.bfloat16, jnp.float32, jnp.int32
NT = (((1,), (1,)), ((), ()))
TN = (((0,), (0,)), ((), ()))
ROOM = 32 * 1024 * 1024


def shifted(block, axis, distance):
    size = lax.axis_size(axis)
    return lax.ppermute(block, axis, [((i - distance) % size, i) for i in range(size)])


def norms_of(floats):
    return jnp.sqrt(jnp.sum(floats * floats, -1, keepdims=True) + EPSILON)


def vmem(count):
    return [pl.BlockSpec(memory_space=pltpu.VMEM)] * count


def iota(shape, dim):
    return lax.broadcasted_iota(i32, shape, dim)


def prepare(pos_ref, text_hbm, ids_hbm, domain_hbm, bias_hbm, out_ref, text_ref, ids_ref, domain_ref, bias_ref, sems):
    pairs = ((text_hbm, text_ref), (ids_hbm, ids_ref), (domain_hbm, domain_ref), (bias_hbm, bias_ref))
    copies = [pltpu.make_async_copy(src, dst, sems.at[k]) for k, (src, dst) in enumerate(pairs)]
    for copy in copies:
        copy.start()
    for copy in copies:
        copy.wait()
    rows, width = text_ref.shape
    floats = text_ref[...].astype(f32)
    out_ref[:, :width] = (floats / norms_of(floats)).astype(bf16)
    wide = (rows, ids_ref.shape[1])
    mine = iota(wide, 1) == iota(wide, 0) + pos_ref[0] * rows
    own_id = jnp.sum(jnp.where(mine, ids_ref[...].astype(f32), 0.0), -1, keepdims=True)
    own_domain = jnp.sum(jnp.where(mine, domain_ref[...].astype(f32), 0.0), -1, keepdims=True)
    table = (rows, bias_ref.shape[1])
    chosen = own_domain.astype(i32) == iota(table, 1)
    bias = jnp.sum(jnp.where(chosen, jnp.broadcast_to(bias_ref[...], table), 0.0), -1, keepdims=True)
    whole = own_id.astype(i32)
    high = (whole >> 6).astype(f32)
    low = (whole & 63).astype(f32)
    first = bias.astype(bf16).astype(f32)
    second = (bias - first).astype(bf16).astype(f32)
    third = bias - first - second
    lane = iota((rows, TAIL), 1)
    tail = jnp.zeros((rows, TAIL), f32)
    for k, part in enumerate((high, low, first, second, third)):
        tail = jnp.where(lane == k, part, tail)
    out_ref[:, width:] = tail.astype(bf16)


def fan_out(feat_ref, _payload, feats_hbm, sem):
    copies = [pltpu.make_async_copy(feat_ref, feats_hbm.at[k], sem) for k in range(feats_hbm.shape[0])]
    for copy in copies:
        copy.start()
    for copy in copies:
        copy.wait()


def assemble(*refs):
    out_ref, count = refs[-1], refs[0].shape[0]
    for k, ref in enumerate(refs[:-1]):
        out_ref[k * count : (k + 1) * count] = ref[...]


def slopes(rows, image_round, ids):
    width = image_round.shape[1]
    images = image_round.shape[0]
    tail = rows[:, width:]
    which = iota((TAIL, images), 0)
    take_id = jnp.where(which == 0, 64.0, jnp.where(which == 1, 1.0, 0.0)).astype(bf16)
    take_bias = jnp.where((which >= 2) & (which < 5), 1.0, 0.0).astype(bf16)
    logits = SCALE * lax.dot_general(rows[:, :width], image_round, NT, preferred_element_type=f32)
    logits = logits + jnp.dot(tail, take_bias, preferred_element_type=f32)
    text_ids = jnp.dot(tail, take_id, preferred_element_type=f32)
    signs = jnp.where(text_ids == ids.astype(f32), 1.0, -1.0)
    return (-signs * jax.nn.sigmoid(-signs * logits)).astype(bf16)


def image_side(pieces, plane_ref, a_ref, b_ref, own_ref, embed_ref, ids_ref, grad_ref, kept_ref, far_ref, *rest):
    turned_refs, turned_f32 = rest[:-1], rest[-1]
    floats = embed_ref[...].astype(f32)
    norms = norms_of(floats)
    units = floats / norms
    rounded = units.astype(bf16)
    width = floats.shape[1]
    total = jnp.zeros(floats.shape, f32)
    for ref in (a_ref, b_ref):
        rows = ref[...]
        slope = slopes(rows, rounded, ids_ref[...])
        total = total + lax.dot_general(slope, rows[:, :width], TN, preferred_element_type=f32)
    total = SCALE * total
    grad = (total - units * jnp.sum(units * total, -1, keepdims=True)) / norms
    grad_ref[...] = grad.astype(bf16)
    turned_f32[...] = grad.T
    planes = len(turned_refs)
    run = width // (planes * pieces)
    for ahead, ref in enumerate(turned_refs):
        plane = lax.rem(plane_ref[0] + ahead, planes)
        parts = [
            turned_f32[pl.ds(pl.multiple_of((p * planes + plane) * run, 8), run)]
            for p in range(pieces)
        ]
        ref[...] = jnp.concatenate(parts, 0).astype(bf16)
    slope = slopes(own_ref[...], rounded, ids_ref[...])
    share = SCALE * jnp.dot(slope, rounded, preferred_element_type=f32)
    half = kept_ref.shape[0]
    kept_ref[...] = share[:half]
    far_ref[...] = share[half:].astype(bf16)


def text_middle(kept_ref, back_ref, _parts, stay_ref, pass_ref):
    count = stay_ref.shape[0]
    total = kept_ref[...] + back_ref[...].astype(f32)
    stay_ref[...] = total[:count]
    pass_ref[...] = total[count:].astype(bf16)


def head_side(plane_ref, feat_ref, *refs):
    out_ref, planes = refs[-1], feat_ref.shape[0]
    refs = refs[:planes]
    part = jnp.zeros((refs[0].shape[0], feat_ref.shape[2]), f32)
    for behind, ref in enumerate(refs):
        plane = lax.rem(plane_ref[0] + (planes - behind), planes)
        part = part + jnp.dot(ref[...], feat_ref[plane], preferred_element_type=f32)
    targets, groups = out_ref.shape[0], part.shape[1] // 128
    run = part.shape[0] // targets
    for c in range(targets):
        for g in range(groups):
            out_ref[c, g * run : (g + 1) * run] = part[
                c * run : (c + 1) * run, g * 128 : (g + 1) * 128
            ].astype(bf16)


def head_sum(parts_ref, out_ref):
    total = jnp.sum(parts_ref[...].astype(f32), 0)
    run, groups = out_ref.shape[0], out_ref.shape[1] // 128
    for g in range(groups):
        out_ref[:, g * 128 : (g + 1) * 128] = total[g * run : (g + 1) * run]


def finish(grad_ref, head_ref, stay_ref, last_ref, text_ref, image_ref, out_ref):
    image_ref[...] = jnp.dot(grad_ref[...], head_ref[...], preferred_element_type=f32).astype(bf16)
    floats = text_ref[...].astype(f32)
    norms = norms_of(floats)
    units = floats / norms
    total = stay_ref[...] + last_ref[...].astype(f32)
    out_ref[...] = (total - units * jnp.sum(units * total, -1, keepdims=True)) / norms


def call(kernel, shapes, *args, smem=0, hbm=0, after=0, out_hbm=0, scratch=(), cost=None, room=None):
    specs = [pl.BlockSpec(memory_space=pltpu.SMEM)] * smem
    specs += [pl.BlockSpec(memory_space=pltpu.HBM)] * hbm
    specs += vmem(len(args) - smem - hbm - after)
    specs += [pl.BlockSpec(memory_space=pl.ANY)] * after
    outs = [jax.ShapeDtypeStruct(s, d) for s, d in shapes]
    out_specs = vmem(len(outs) - out_hbm) + [pl.BlockSpec(memory_space=pltpu.HBM)] * out_hbm
    single = len(outs) == 1
    return pl.pallas_call(
        kernel,
        out_shape=outs[0] if single else outs,
        in_specs=specs,
        out_specs=out_specs[0] if single else out_specs,
        scratch_shapes=list(scratch),
        compiler_params=pltpu.CompilerParams(vmem_limit_bytes=room),
        cost_estimate=cost,
        name=getattr(kernel, "func", kernel).__name__,
    )(*args)


def lasting(us):
    return pl.CostEstimate(flops=int(us * 1e9), bytes_accessed=0, transcendentals=0)


def local(image_embed, text_embed, image_feat, head, sample_id, domain, domain_bias):
    images, width = image_embed.shape
    texts = text_embed.shape[0]
    features = image_feat.shape[1]
    position = lax.axis_index(TOWER).astype(i32).reshape(1)
    ids = sample_id.reshape(1, images)
    planes = lax.axis_size("z")
    across = lax.axis_size("xh") * lax.axis_size("y")
    own_width = width // planes

    inputs = (text_embed, ids, domain.reshape(1, images), domain_bias.reshape(1, -1))
    payload = call(
        prepare, [((texts, width + TAIL), bf16)], position, *inputs, smem=1, hbm=4,
        scratch=[pltpu.VMEM(v.shape, v.dtype) for v in inputs] + [pltpu.SemaphoreType.DMA((4,))],
    )
    feats = call(
        fan_out, [((planes, images, features), bf16)], image_feat, payload,
        after=1, out_hbm=1, scratch=[pltpu.SemaphoreType.DMA], cost=lasting(20),
    )
    feats = lax.all_to_all(feats, "z", 0, 0, tiled=True)

    window = [payload] + [shifted(payload, BLK, d) for d in (1, 2, 3)]
    own = call(
        assemble, [((len(window) * texts, width + TAIL), bf16)], *window,
        cost=lasting(400), room=ROOM,
    )

    here = lax.all_gather(own, "xl", axis=0, tiled=True)
    there = shifted(here, "core", 1)

    plane = lax.axis_index("z").astype(i32).reshape(1)
    embed_grad, kept, far, *turned = call(
        functools.partial(image_side, lax.axis_size("xh")),
        [((images, width), bf16), ((2 * texts, width), f32), ((2 * texts, width), bf16)]
        + [((own_width, images), bf16)] * planes,
        plane, here, there, own, image_embed, ids, smem=1, room=ROOM,
        scratch=[pltpu.VMEM((width, images), f32)],
    )
    came = turned[:1] + [shifted(turned[d], "z", d) for d in range(1, planes)]

    back = shifted(far, BLK, -2)

    rows = own_width // across
    parts = call(
        head_side, [((across, rows * features // 128, 128), bf16)],
        plane, feats, *came, back, smem=1, after=1, room=ROOM,
    )
    stay, passed = call(
        text_middle, [((texts, width), f32), ((texts, width), bf16)],
        kept, back, parts, after=1, room=ROOM,
    )
    last = shifted(passed, BLK, -1)
    parts = lax.all_to_all(parts, ("xh", "y"), 0, 0, tiled=True)
    image_grad, text_grad = call(
        finish, [((images, features), bf16), ((texts, width), f32)],
        embed_grad, head, stay, last, text_embed, cost=lasting(1), room=ROOM,
    )
    head_grad = call(head_sum, [((rows, features), f32)], parts, room=ROOM)
    return (image_grad, text_grad, head_grad)


def solution(mesh):
    split = Mesh(mesh.devices.reshape([n for _, n in SPLIT]), [name for name, _ in SPLIT])
    in_specs = (
        P(BLK, None),
        P(ALL, None),
        P(BLK, TOWER),
        P(None, TOWER),
        P(BLK),
        P(BLK),
        P(),
    )
    out_specs = (P(BLK, TOWER), P(ALL, None), P(BLK, TOWER))
    return jax.shard_map(local, mesh=split, in_specs=in_specs, out_specs=out_specs, check_vma=False)
```

```python
import jax
import jax.numpy as jnp
from jax import lax
from jax.experimental import pallas as pl
from jax.experimental.pallas import tpu as pltpu
from jax.sharding import Mesh, PartitionSpec as P

EPSILON = 1e-06
SCALE = 10.0
TAIL = 128
SPLIT = (("xh", 2), ("z", 8), ("y", 8), ("xl", 4), ("core", 2))
BLK = ("xh", "z", "y")
TOWER = ("xl", "core")
ALL = BLK + TOWER

bf16, f32, i32 = jnp.bfloat16, jnp.float32, jnp.int32
NT = (((1,), (1,)), ((), ()))
TN = (((0,), (0,)), ((), ()))
ROOM = 32 * 1024 * 1024


def shifted(block, axis, distance):
    size = lax.axis_size(axis)
    return lax.ppermute(block, axis, [((i - distance) % size, i) for i in range(size)])


def norms_of(floats):
    return jnp.sqrt(jnp.sum(floats * floats, -1, keepdims=True) + EPSILON)


def vmem(count):
    return [pl.BlockSpec(memory_space=pltpu.VMEM)] * count


def iota(shape, dim):
    return lax.broadcasted_iota(i32, shape, dim)


def prepare(pos_ref, text_hbm, ids_hbm, domain_hbm, bias_hbm, out_ref, text_ref, ids_ref, domain_ref, bias_ref, sems):
    pairs = ((text_hbm, text_ref), (ids_hbm, ids_ref), (domain_hbm, domain_ref), (bias_hbm, bias_ref))
    copies = [pltpu.make_async_copy(src, dst, sems.at[k]) for k, (src, dst) in enumerate(pairs)]
    for copy in copies:
        copy.start()
    for copy in copies:
        copy.wait()
    rows, width = text_ref.shape
    floats = text_ref[...].astype(f32)
    out_ref[:, :width] = (floats / norms_of(floats)).astype(bf16)
    wide = (rows, ids_ref.shape[1])
    mine = iota(wide, 1) == iota(wide, 0) + pos_ref[0] * rows
    own_id = jnp.sum(jnp.where(mine, ids_ref[...].astype(f32), 0.0), -1, keepdims=True)
    own_domain = jnp.sum(jnp.where(mine, domain_ref[...].astype(f32), 0.0), -1, keepdims=True)
    table = (rows, bias_ref.shape[1])
    chosen = own_domain.astype(i32) == iota(table, 1)
    bias = jnp.sum(jnp.where(chosen, jnp.broadcast_to(bias_ref[...], table), 0.0), -1, keepdims=True)
    whole = own_id.astype(i32)
    high = (whole >> 6).astype(f32)
    low = (whole & 63).astype(f32)
    first = bias.astype(bf16).astype(f32)
    second = (bias - first).astype(bf16).astype(f32)
    third = bias - first - second
    lane = iota((rows, TAIL), 1)
    tail = jnp.zeros((rows, TAIL), f32)
    for k, part in enumerate((high, low, first, second, third)):
        tail = jnp.where(lane == k, part, tail)
    out_ref[:, width:] = tail.astype(bf16)


def fan_out(feat_ref, _payload, feats_hbm, sem):
    copies = [pltpu.make_async_copy(feat_ref, feats_hbm.at[k], sem) for k in range(feats_hbm.shape[0])]
    for copy in copies:
        copy.start()
    for copy in copies:
        copy.wait()


def assemble(*refs):
    out_ref, count = refs[-1], refs[0].shape[0]
    for k, ref in enumerate(refs[:-1]):
        out_ref[k * count : (k + 1) * count] = ref[...]


def slopes(rows, image_round, ids):
    width = image_round.shape[1]
    images = image_round.shape[0]
    tail = rows[:, width:]
    which = iota((TAIL, images), 0)
    take_id = jnp.where(which == 0, 64.0, jnp.where(which == 1, 1.0, 0.0)).astype(bf16)
    take_bias = jnp.where((which >= 2) & (which < 5), 1.0, 0.0).astype(bf16)
    logits = SCALE * lax.dot_general(rows[:, :width], image_round, NT, preferred_element_type=f32)
    logits = logits + jnp.dot(tail, take_bias, preferred_element_type=f32)
    text_ids = jnp.dot(tail, take_id, preferred_element_type=f32)
    signs = jnp.where(text_ids == ids.astype(f32), 1.0, -1.0)
    return (-signs * jax.nn.sigmoid(-signs * logits)).astype(bf16)


def image_side(a_ref, b_ref, own_ref, embed_ref, ids_ref, grad_ref, kept_ref, far_ref, turned_ref):
    floats = embed_ref[...].astype(f32)
    norms = norms_of(floats)
    units = floats / norms
    rounded = units.astype(bf16)
    width = floats.shape[1]
    total = jnp.zeros(floats.shape, f32)
    for ref in (a_ref, b_ref):
        rows = ref[...]
        slope = slopes(rows, rounded, ids_ref[...])
        total = total + lax.dot_general(slope, rows[:, :width], TN, preferred_element_type=f32)
    total = SCALE * total
    grad = (total - units * jnp.sum(units * total, -1, keepdims=True)) / norms
    grad_ref[...] = grad.astype(bf16)
    turned = grad.T.astype(bf16)
    planes, pieces, run = turned_ref.shape[:3]
    for p in range(pieces):
        for z in range(planes):
            start = (p * planes + z) * run
            turned_ref[z, p] = turned[start : start + run]
    slope = slopes(own_ref[...], rounded, ids_ref[...])
    share = SCALE * jnp.dot(slope, rounded, preferred_element_type=f32)
    half = kept_ref.shape[0]
    kept_ref[...] = share[:half]
    far_ref[...] = share[half:].astype(bf16)


def text_middle(kept_ref, back_ref, _parts, stay_ref, pass_ref):
    count = stay_ref.shape[0]
    total = kept_ref[...] + back_ref[...].astype(f32)
    stay_ref[...] = total[:count]
    pass_ref[...] = total[count:].astype(bf16)


def head_side(turned_ref, feat_ref, _back, out_ref):
    part = jnp.zeros((turned_ref.shape[1], feat_ref.shape[2]), f32)
    for k in range(turned_ref.shape[0]):
        part = part + jnp.dot(turned_ref[k], feat_ref[k], preferred_element_type=f32)
    targets, groups = out_ref.shape[0], part.shape[1] // 128
    run = part.shape[0] // targets
    for c in range(targets):
        for g in range(groups):
            out_ref[c, g * run : (g + 1) * run] = part[
                c * run : (c + 1) * run, g * 128 : (g + 1) * 128
            ].astype(bf16)


def head_sum(parts_ref, out_ref):
    total = jnp.sum(parts_ref[...].astype(f32), 0)
    run, groups = out_ref.shape[0], out_ref.shape[1] // 128
    for g in range(groups):
        out_ref[:, g * 128 : (g + 1) * 128] = total[g * run : (g + 1) * run]


def text_back(stay_ref, last_ref, text_ref, out_ref):
    floats = text_ref[...].astype(f32)
    norms = norms_of(floats)
    units = floats / norms
    total = stay_ref[...] + last_ref[...].astype(f32)
    out_ref[...] = (total - units * jnp.sum(units * total, -1, keepdims=True)) / norms


def call(kernel, shapes, *args, smem=0, hbm=0, after=0, out_hbm=0, scratch=(), cost=None, room=None):
    specs = [pl.BlockSpec(memory_space=pltpu.SMEM)] * smem
    specs += [pl.BlockSpec(memory_space=pltpu.HBM)] * hbm
    specs += vmem(len(args) - smem - hbm - after)
    specs += [pl.BlockSpec(memory_space=pl.ANY)] * after
    outs = [jax.ShapeDtypeStruct(s, d) for s, d in shapes]
    out_specs = vmem(len(outs) - out_hbm) + [pl.BlockSpec(memory_space=pltpu.HBM)] * out_hbm
    single = len(outs) == 1
    return pl.pallas_call(
        kernel,
        out_shape=outs[0] if single else outs,
        in_specs=specs,
        out_specs=out_specs[0] if single else out_specs,
        scratch_shapes=list(scratch),
        compiler_params=pltpu.CompilerParams(vmem_limit_bytes=room),
        cost_estimate=cost,
        name=kernel.__name__,
    )(*args)


def lasting(us):
    return pl.CostEstimate(flops=int(us * 1e9), bytes_accessed=0, transcendentals=0)


def local(image_embed, text_embed, image_feat, head, sample_id, domain, domain_bias):
    images, width = image_embed.shape
    texts = text_embed.shape[0]
    features = image_feat.shape[1]
    position = lax.axis_index(TOWER).astype(i32).reshape(1)
    ids = sample_id.reshape(1, images)
    planes = lax.axis_size("z")
    across = lax.axis_size("xh") * lax.axis_size("y")
    own_width = width // planes

    inputs = (text_embed, ids, domain.reshape(1, images), domain_bias.reshape(1, -1))
    payload = call(
        prepare, [((texts, width + TAIL), bf16)], position, *inputs, smem=1, hbm=4,
        scratch=[pltpu.VMEM(v.shape, v.dtype) for v in inputs] + [pltpu.SemaphoreType.DMA((4,))],
    )
    feats = call(
        fan_out, [((planes, images, features), bf16)], image_feat, payload,
        after=1, out_hbm=1, scratch=[pltpu.SemaphoreType.DMA],
    )
    feats = lax.all_to_all(feats, "z", 0, 0, tiled=True)

    window = [payload] + [shifted(payload, BLK, d) for d in (1, 2, 3)]
    own = call(
        assemble, [((len(window) * texts, width + TAIL), bf16)], *window,
        room=ROOM,
    )

    here = lax.all_gather(own, "xl", axis=0, tiled=True)
    there = shifted(here, "core", 1)

    pieces = lax.axis_size("xh")
    run = width // (planes * pieces)
    embed_grad, kept, far, turned = call(
        image_side,
        [((images, width), bf16), ((2 * texts, width), f32), ((2 * texts, width), bf16),
         ((planes, pieces, run, images), bf16)],
        here, there, own, image_embed, ids, room=ROOM,
    )
    turned, feats = lax.optimization_barrier((turned, feats))
    plane = lax.all_to_all(turned.reshape(planes, own_width, images), "z", 0, 0, tiled=True)

    back = shifted(far, BLK, -2)

    rows = own_width // across
    parts = call(
        head_side, [((across, rows * features // 128, 128), bf16)],
        plane, feats, back, after=1,
    )
    stay, passed = call(
        text_middle, [((texts, width), f32), ((texts, width), bf16)],
        kept, back, parts, after=1, room=ROOM,
    )
    last = shifted(passed, BLK, -1)
    parts = lax.all_to_all(parts, ("xh", "y"), 0, 0, tiled=True)
    image_grad = jnp.dot(embed_grad, head, preferred_element_type=f32).astype(bf16)
    text_grad = call(
        text_back, [((texts, width), f32)], stay, last, text_embed, cost=lasting(1), room=ROOM
    )
    head_grad = call(head_sum, [((rows, features), f32)], parts, room=ROOM)
    return (image_grad, text_grad, head_grad)


def solution(mesh):
    split = Mesh(mesh.devices.reshape([n for _, n in SPLIT]), [name for name, _ in SPLIT])
    in_specs = (
        P(BLK, None),
        P(ALL, None),
        P(BLK, TOWER),
        P(None, TOWER),
        P(BLK),
        P(BLK),
        P(),
    )
    out_specs = (P(BLK, TOWER), P(ALL, None), P(BLK, TOWER))
    return jax.shard_map(local, mesh=split, in_specs=in_specs, out_specs=out_specs, check_vma=False)
```

```python
import jax
import jax.numpy as jnp
from jax import lax
from jax.experimental import pallas as pl
from jax.experimental.pallas import tpu as pltpu
from jax.sharding import Mesh, PartitionSpec as P

EPSILON = 1e-06
SCALE = 10.0
TAIL = 128
SPLIT = (("xh", 2), ("z", 8), ("y", 8), ("xl", 4), ("core", 2))
BLK = ("xh", "z", "y")
TOWER = ("xl", "core")
ALL = BLK + TOWER

bf16, f32, i32 = jnp.bfloat16, jnp.float32, jnp.int32
NT = (((1,), (1,)), ((), ()))
TN = (((0,), (0,)), ((), ()))
ROOM = 32 * 1024 * 1024


def shifted(block, axis, distance):
    size = lax.axis_size(axis)
    return lax.ppermute(block, axis, [((i - distance) % size, i) for i in range(size)])


def norms_of(floats):
    return jnp.sqrt(jnp.sum(floats * floats, -1, keepdims=True) + EPSILON)


def vmem(count):
    return [pl.BlockSpec(memory_space=pltpu.VMEM)] * count


def iota(shape, dim):
    return lax.broadcasted_iota(i32, shape, dim)


def prepare(pos_ref, text_hbm, ids_hbm, domain_hbm, bias_hbm, out_ref, text_ref, ids_ref, domain_ref, bias_ref, sems):
    pairs = ((text_hbm, text_ref), (ids_hbm, ids_ref), (domain_hbm, domain_ref), (bias_hbm, bias_ref))
    copies = [pltpu.make_async_copy(src, dst, sems.at[k]) for k, (src, dst) in enumerate(pairs)]
    for copy in copies:
        copy.start()
    for copy in copies:
        copy.wait()
    rows, width = text_ref.shape
    floats = text_ref[...].astype(f32)
    out_ref[:, :width] = (floats / norms_of(floats)).astype(bf16)
    wide = (rows, ids_ref.shape[1])
    mine = iota(wide, 1) == iota(wide, 0) + pos_ref[0] * rows
    own_id = jnp.sum(jnp.where(mine, ids_ref[...].astype(f32), 0.0), -1, keepdims=True)
    own_domain = jnp.sum(jnp.where(mine, domain_ref[...].astype(f32), 0.0), -1, keepdims=True)
    table = (rows, bias_ref.shape[1])
    chosen = own_domain.astype(i32) == iota(table, 1)
    bias = jnp.sum(jnp.where(chosen, jnp.broadcast_to(bias_ref[...], table), 0.0), -1, keepdims=True)
    whole = own_id.astype(i32)
    high = (whole >> 6).astype(f32)
    low = (whole & 63).astype(f32)
    first = bias.astype(bf16).astype(f32)
    second = (bias - first).astype(bf16).astype(f32)
    third = bias - first - second
    lane = iota((rows, TAIL), 1)
    tail = jnp.zeros((rows, TAIL), f32)
    for k, part in enumerate((high, low, first, second, third)):
        tail = jnp.where(lane == k, part, tail)
    out_ref[:, width:] = tail.astype(bf16)


def fan_out(feat_ref, _payload, feats_hbm, sem):
    copies = [pltpu.make_async_copy(feat_ref, feats_hbm.at[k], sem) for k in range(feats_hbm.shape[0])]
    for copy in copies:
        copy.start()
    for copy in copies:
        copy.wait()


def assemble(*refs):
    out_ref, count = refs[-1], refs[0].shape[0]
    for k, ref in enumerate(refs[:-1]):
        out_ref[k * count : (k + 1) * count] = ref[...]


def slopes(rows, image_round, ids):
    width = image_round.shape[1]
    images = image_round.shape[0]
    tail = rows[:, width:]
    which = iota((TAIL, images), 0)
    take_id = jnp.where(which == 0, 64.0, jnp.where(which == 1, 1.0, 0.0)).astype(bf16)
    take_bias = jnp.where((which >= 2) & (which < 5), 1.0, 0.0).astype(bf16)
    logits = SCALE * lax.dot_general(rows[:, :width], image_round, NT, preferred_element_type=f32)
    logits = logits + jnp.dot(tail, take_bias, preferred_element_type=f32)
    text_ids = jnp.dot(tail, take_id, preferred_element_type=f32)
    signs = jnp.where(text_ids == ids.astype(f32), 1.0, -1.0)
    return (-signs * jax.nn.sigmoid(-signs * logits)).astype(bf16)


def image_side(a_ref, b_ref, own_ref, embed_ref, ids_ref, grad_ref, turned_ref, *share_refs):
    floats = embed_ref[...].astype(f32)
    norms = norms_of(floats)
    units = floats / norms
    rounded = units.astype(bf16)
    width = floats.shape[1]
    total = jnp.zeros(floats.shape, f32)
    for ref in (a_ref, b_ref):
        rows = ref[...]
        slope = slopes(rows, rounded, ids_ref[...])
        total = total + lax.dot_general(slope, rows[:, :width], TN, preferred_element_type=f32)
    total = SCALE * total
    grad = (total - units * jnp.sum(units * total, -1, keepdims=True)) / norms
    grad_ref[...] = grad.astype(bf16)
    turned = grad.T.astype(bf16)
    planes, pieces, run = turned_ref.shape[:3]
    for p in range(pieces):
        for z in range(planes):
            start = (p * planes + z) * run
            turned_ref[z, p] = turned[start : start + run]
    slope = slopes(own_ref[...], rounded, ids_ref[...])
    share = SCALE * jnp.dot(slope, rounded, preferred_element_type=f32)
    count = share_refs[0].shape[0]
    for k, ref in enumerate(share_refs):
        ref[...] = share[k * count : (k + 1) * count].astype(ref.dtype)


def head_side(feat_ref, turned_ref, out_ref):
    part = jnp.zeros((turned_ref.shape[1], feat_ref.shape[2]), f32)
    for k in range(turned_ref.shape[0]):
        part = part + jnp.dot(turned_ref[k], feat_ref[k], preferred_element_type=f32)
    targets, groups = out_ref.shape[0], part.shape[1] // 128
    run = part.shape[0] // targets
    for c in range(targets):
        for g in range(groups):
            out_ref[c, g * run : (g + 1) * run] = part[
                c * run : (c + 1) * run, g * 128 : (g + 1) * 128
            ].astype(bf16)


def head_sum(parts_ref, out_ref):
    total = jnp.sum(parts_ref[...].astype(f32), 0)
    run, groups = out_ref.shape[0], out_ref.shape[1] // 128
    for g in range(groups):
        out_ref[:, g * 128 : (g + 1) * 128] = total[g * run : (g + 1) * run]


def finish(grad_ref, head_ref, text_ref, kept_ref, one_ref, two_ref, three_ref, image_ref, out_ref):
    image_ref[...] = jnp.dot(grad_ref[...], head_ref[...], preferred_element_type=f32).astype(bf16)
    floats = text_ref[...].astype(f32)
    norms = norms_of(floats)
    units = floats / norms
    total = kept_ref[...]
    for ref in (one_ref, two_ref, three_ref):
        total = total + ref[...].astype(f32)
    out_ref[...] = (total - units * jnp.sum(units * total, -1, keepdims=True)) / norms


def call(kernel, shapes, *args, smem=0, hbm=0, after=0, out_hbm=0, scratch=(), cost=None, room=None):
    specs = [pl.BlockSpec(memory_space=pltpu.SMEM)] * smem
    specs += [pl.BlockSpec(memory_space=pltpu.HBM)] * hbm
    specs += vmem(len(args) - smem - hbm - after)
    specs += [pl.BlockSpec(memory_space=pl.ANY)] * after
    outs = [jax.ShapeDtypeStruct(s, d) for s, d in shapes]
    out_specs = vmem(len(outs) - out_hbm) + [pl.BlockSpec(memory_space=pltpu.HBM)] * out_hbm
    single = len(outs) == 1
    return pl.pallas_call(
        kernel,
        out_shape=outs[0] if single else outs,
        in_specs=specs,
        out_specs=out_specs[0] if single else out_specs,
        scratch_shapes=list(scratch),
        compiler_params=pltpu.CompilerParams(vmem_limit_bytes=room),
        cost_estimate=cost,
        name=kernel.__name__,
    )(*args)


def lasting(us):
    return pl.CostEstimate(flops=int(us * 1e9), bytes_accessed=0, transcendentals=0)


def local(image_embed, text_embed, image_feat, head, sample_id, domain, domain_bias):
    images, width = image_embed.shape
    texts = text_embed.shape[0]
    features = image_feat.shape[1]
    position = lax.axis_index(TOWER).astype(i32).reshape(1)
    ids = sample_id.reshape(1, images)
    planes = lax.axis_size("z")
    across = lax.axis_size("xh") * lax.axis_size("y")
    own_width = width // planes

    inputs = (text_embed, ids, domain.reshape(1, images), domain_bias.reshape(1, -1))
    payload = call(
        prepare, [((texts, width + TAIL), bf16)], position, *inputs, smem=1, hbm=4,
        scratch=[pltpu.VMEM(v.shape, v.dtype) for v in inputs] + [pltpu.SemaphoreType.DMA((4,))],
    )
    feats = call(
        fan_out, [((planes, images, features), bf16)], image_feat, payload,
        after=1, out_hbm=1, scratch=[pltpu.SemaphoreType.DMA],
    )
    feats = lax.all_to_all(feats, "z", 0, 0, tiled=True)

    window = [payload] + [shifted(payload, BLK, d) for d in (1, 2, 3)]
    own = call(
        assemble, [((len(window) * texts, width + TAIL), bf16)], *window,
        room=ROOM,
    )

    here = lax.all_gather(own, "xl", axis=0, tiled=True)
    there = shifted(here, "core", 1)

    pieces = lax.axis_size("xh")
    run = width // (planes * pieces)
    embed_grad, turned, kept, *aways = call(
        image_side,
        [((images, width), bf16), ((planes, pieces, run, images), bf16), ((texts, width), f32)]
        + [((texts, width), bf16)] * 3,
        here, there, own, image_embed, ids, room=ROOM,
    )
    turned, feats = lax.optimization_barrier((turned, feats))
    plane = lax.all_to_all(turned.reshape(planes, own_width, images), "z", 0, 0, tiled=True)

    backs = [shifted(away, BLK, -d) for d, away in zip((1, 2, 3), aways)]

    rows = own_width // across
    parts = call(
        head_side, [((across, rows * features // 128, 128), bf16)], feats, plane, room=ROOM,
    )
    parts = lax.all_to_all(parts, ("xh", "y"), 0, 0, tiled=True)
    image_grad, text_grad = call(
        finish, [((images, features), bf16), ((texts, width), f32)],
        embed_grad, head, text_embed, kept, *backs, cost=lasting(60), room=ROOM,
    )
    head_grad = call(head_sum, [((rows, features), f32)], parts, room=ROOM)
    return (image_grad, text_grad, head_grad)


def solution(mesh):
    split = Mesh(mesh.devices.reshape([n for _, n in SPLIT]), [name for name, _ in SPLIT])
    in_specs = (
        P(BLK, None),
        P(ALL, None),
        P(BLK, TOWER),
        P(None, TOWER),
        P(BLK),
        P(BLK),
        P(),
    )
    out_specs = (P(BLK, TOWER), P(ALL, None), P(BLK, TOWER))
    return jax.shard_map(local, mesh=split, in_specs=in_specs, out_specs=out_specs, check_vma=False)
```

```python
import jax
import jax.numpy as jnp
from jax import lax
from jax.experimental import pallas as pl
from jax.experimental.pallas import tpu as pltpu
from jax.sharding import Mesh, PartitionSpec as P

EPSILON = 1e-06
SCALE = 10.0
TAIL = 128
SPLIT = (("xh", 2), ("z", 8), ("y", 8), ("xl", 4), ("core", 2))
BLK = ("xh", "z", "y")
TOWER = ("xl", "core")
ALL = BLK + TOWER

bf16, f32, i32 = jnp.bfloat16, jnp.float32, jnp.int32
NT = (((1,), (1,)), ((), ()))
TN = (((0,), (0,)), ((), ()))
ROOM = 32 * 1024 * 1024


def shifted(block, axis, distance):
    size = lax.axis_size(axis)
    return lax.ppermute(block, axis, [((i - distance) % size, i) for i in range(size)])


def norms_of(floats):
    return jnp.sqrt(jnp.sum(floats * floats, -1, keepdims=True) + EPSILON)


def vmem(count):
    return [pl.BlockSpec(memory_space=pltpu.VMEM)] * count


def iota(shape, dim):
    return lax.broadcasted_iota(i32, shape, dim)


def prepare(pos_ref, *refs):
    sources, (out_ref, feats_hbm), held, sems, sem = refs[:5], refs[5:7], refs[7:12], refs[12], refs[13]
    copies = [pltpu.make_async_copy(src, dst, sems.at[k]) for k, (src, dst) in enumerate(zip(sources, held))]
    for copy in copies:
        copy.start()
    text_ref, ids_ref, domain_ref, bias_ref, feat_ref = held
    fans = [pltpu.make_async_copy(feat_ref, feats_hbm.at[k], sem.at[k]) for k in range(feats_hbm.shape[0])]
    copies[4].wait()
    for fan in fans:
        fan.start()
    for copy in copies[:4]:
        copy.wait()
    rows, width = text_ref.shape
    floats = text_ref[...].astype(f32)
    out_ref[:, :width] = (floats / norms_of(floats)).astype(bf16)
    wide = (rows, ids_ref.shape[1])
    mine = iota(wide, 1) == iota(wide, 0) + pos_ref[0] * rows
    own_id = jnp.sum(jnp.where(mine, ids_ref[...].astype(f32), 0.0), -1, keepdims=True)
    own_domain = jnp.sum(jnp.where(mine, domain_ref[...].astype(f32), 0.0), -1, keepdims=True)
    table = (rows, bias_ref.shape[1])
    chosen = own_domain.astype(i32) == iota(table, 1)
    bias = jnp.sum(jnp.where(chosen, jnp.broadcast_to(bias_ref[...], table), 0.0), -1, keepdims=True)
    whole = own_id.astype(i32)
    high = (whole >> 6).astype(f32)
    low = (whole & 63).astype(f32)
    first = bias.astype(bf16).astype(f32)
    second = (bias - first).astype(bf16).astype(f32)
    third = bias - first - second
    lane = iota((rows, TAIL), 1)
    tail = jnp.zeros((rows, TAIL), f32)
    for k, part in enumerate((high, low, first, second, third)):
        tail = jnp.where(lane == k, part, tail)
    out_ref[:, width:] = tail.astype(bf16)
    for fan in fans:
        fan.wait()


def assemble(*refs):
    out_ref, count = refs[-1], refs[0].shape[0]
    for k, ref in enumerate(refs[:-1]):
        out_ref[k * count : (k + 1) * count] = ref[...]


def slopes(rows, image_round, ids):
    width = image_round.shape[1]
    images = image_round.shape[0]
    tail = rows[:, width:]
    which = iota((TAIL, images), 0)
    take_id = jnp.where(which == 0, 64.0, jnp.where(which == 1, 1.0, 0.0)).astype(bf16)
    take_bias = jnp.where((which >= 2) & (which < 5), 1.0, 0.0).astype(bf16)
    logits = SCALE * lax.dot_general(rows[:, :width], image_round, NT, preferred_element_type=f32)
    logits = logits + jnp.dot(tail, take_bias, preferred_element_type=f32)
    text_ids = jnp.dot(tail, take_id, preferred_element_type=f32)
    signs = jnp.where(text_ids == ids.astype(f32), 1.0, -1.0)
    return (-signs * jax.nn.sigmoid(-signs * logits)).astype(bf16)


def image_side(a_ref, b_ref, own_ref, embed_ref, ids_ref, grad_ref, turned_ref, *share_refs):
    floats = embed_ref[...].astype(f32)
    norms = norms_of(floats)
    units = floats / norms
    rounded = units.astype(bf16)
    width = floats.shape[1]
    total = jnp.zeros(floats.shape, f32)
    for ref in (a_ref, b_ref):
        rows = ref[...]
        slope = slopes(rows, rounded, ids_ref[...])
        total = total + lax.dot_general(slope, rows[:, :width], TN, preferred_element_type=f32)
    total = SCALE * total
    grad = (total - units * jnp.sum(units * total, -1, keepdims=True)) / norms
    grad_ref[...] = grad.astype(bf16)
    turned = grad.T.astype(bf16)
    planes, pieces, run = turned_ref.shape[:3]
    for p in range(pieces):
        for z in range(planes):
            start = (p * planes + z) * run
            turned_ref[z, p] = turned[start : start + run]
    slope = slopes(own_ref[...], rounded, ids_ref[...])
    share = SCALE * jnp.dot(slope, rounded, preferred_element_type=f32)
    count = share_refs[0].shape[0]
    for k, ref in enumerate(share_refs):
        ref[...] = share[k * count : (k + 1) * count].astype(ref.dtype)


def head_side(feat_ref, turned_ref, out_ref):
    part = jnp.zeros((turned_ref.shape[1], feat_ref.shape[2]), f32)
    for k in range(turned_ref.shape[0]):
        part = part + jnp.dot(turned_ref[k], feat_ref[k], preferred_element_type=f32)
    targets, groups = out_ref.shape[0], part.shape[1] // 128
    run = part.shape[0] // targets
    for c in range(targets):
        for g in range(groups):
            out_ref[c, g * run : (g + 1) * run] = part[
                c * run : (c + 1) * run, g * 128 : (g + 1) * 128
            ].astype(bf16)


def head_sum(parts_ref, out_ref):
    total = jnp.sum(parts_ref[...].astype(f32), 0)
    run, groups = out_ref.shape[0], out_ref.shape[1] // 128
    for g in range(groups):
        out_ref[:, g * 128 : (g + 1) * 128] = total[g * run : (g + 1) * run]


def finish(grad_ref, head_ref, text_ref, kept_ref, one_ref, two_ref, three_ref, image_ref, out_ref):
    image_ref[...] = jnp.dot(grad_ref[...], head_ref[...], preferred_element_type=f32).astype(bf16)
    floats = text_ref[...].astype(f32)
    norms = norms_of(floats)
    units = floats / norms
    total = kept_ref[...]
    for ref in (one_ref, two_ref, three_ref):
        total = total + ref[...].astype(f32)
    out_ref[...] = (total - units * jnp.sum(units * total, -1, keepdims=True)) / norms


def call(kernel, shapes, *args, smem=0, hbm=0, after=0, out_hbm=0, scratch=(), cost=None, room=None):
    specs = [pl.BlockSpec(memory_space=pltpu.SMEM)] * smem
    specs += [pl.BlockSpec(memory_space=pltpu.HBM)] * hbm
    specs += vmem(len(args) - smem - hbm - after)
    specs += [pl.BlockSpec(memory_space=pl.ANY)] * after
    outs = [jax.ShapeDtypeStruct(s, d) for s, d in shapes]
    out_specs = vmem(len(outs) - out_hbm) + [pl.BlockSpec(memory_space=pltpu.HBM)] * out_hbm
    single = len(outs) == 1
    return pl.pallas_call(
        kernel,
        out_shape=outs[0] if single else outs,
        in_specs=specs,
        out_specs=out_specs[0] if single else out_specs,
        scratch_shapes=list(scratch),
        compiler_params=pltpu.CompilerParams(vmem_limit_bytes=room),
        cost_estimate=cost,
        name=kernel.__name__,
    )(*args)


def lasting(us):
    return pl.CostEstimate(flops=int(us * 1e9), bytes_accessed=0, transcendentals=0)


def local(image_embed, text_embed, image_feat, head, sample_id, domain, domain_bias):
    images, width = image_embed.shape
    texts = text_embed.shape[0]
    features = image_feat.shape[1]
    position = lax.axis_index(TOWER).astype(i32).reshape(1)
    ids = sample_id.reshape(1, images)
    planes = lax.axis_size("z")
    across = lax.axis_size("xh") * lax.axis_size("y")
    own_width = width // planes

    inputs = (text_embed, ids, domain.reshape(1, images), domain_bias.reshape(1, -1), image_feat)
    payload, feats = call(
        prepare, [((texts, width + TAIL), bf16), ((planes, images, features), bf16)],
        position, *inputs, smem=1, hbm=5, out_hbm=1,
        scratch=[pltpu.VMEM(v.shape, v.dtype) for v in inputs]
        + [pltpu.SemaphoreType.DMA((5,)), pltpu.SemaphoreType.DMA((planes,))],
    )
    feats = lax.all_to_all(feats, "z", 0, 0, tiled=True)

    window = [payload] + [shifted(payload, BLK, d) for d in (1, 2, 3)]
    own = call(
        assemble, [((len(window) * texts, width + TAIL), bf16)], *window,
        room=ROOM,
    )

    here = lax.all_gather(own, "xl", axis=0, tiled=True)
    there = shifted(here, "core", 1)

    pieces = lax.axis_size("xh")
    run = width // (planes * pieces)
    embed_grad, turned, kept, *aways = call(
        image_side,
        [((images, width), bf16), ((planes, pieces, run, images), bf16), ((texts, width), f32)]
        + [((texts, width), bf16)] * 3,
        here, there, own, image_embed, ids, room=ROOM,
    )
    turned, feats = lax.optimization_barrier((turned, feats))
    plane = lax.all_to_all(turned.reshape(planes, own_width, images), "z", 0, 0, tiled=True)

    backs = [shifted(away, BLK, -d) for d, away in zip((1, 2, 3), aways)]

    rows = own_width // across
    parts = call(
        head_side, [((across, rows * features // 128, 128), bf16)], feats, plane, room=ROOM,
    )
    parts = lax.all_to_all(parts, ("xh", "y"), 0, 0, tiled=True)
    image_grad, text_grad = call(
        finish, [((images, features), bf16), ((texts, width), f32)],
        embed_grad, head, text_embed, kept, *backs, cost=lasting(60), room=ROOM,
    )
    head_grad = call(head_sum, [((rows, features), f32)], parts, room=ROOM)
    return (image_grad, text_grad, head_grad)


def solution(mesh):
    split = Mesh(mesh.devices.reshape([n for _, n in SPLIT]), [name for name, _ in SPLIT])
    in_specs = (
        P(BLK, None),
        P(ALL, None),
        P(BLK, TOWER),
        P(None, TOWER),
        P(BLK),
        P(BLK),
        P(),
    )
    out_specs = (P(BLK, TOWER), P(ALL, None), P(BLK, TOWER))
    return jax.shard_map(local, mesh=split, in_specs=in_specs, out_specs=out_specs, check_vma=False)
```

```python
import functools

import jax
import jax.numpy as jnp
from jax import lax
from jax.experimental import pallas as pl
from jax.experimental.pallas import tpu as pltpu
from jax.sharding import Mesh, PartitionSpec as P

EPSILON = 1e-06
SCALE = 10.0
TAIL = 128
SPLIT = (("xh", 2), ("z", 8), ("y", 8), ("xl", 4), ("core", 2))
BLK = ("xh", "z", "y")
TOWER = ("xl", "core")
ALL = BLK + TOWER

bf16, f32, i32 = jnp.bfloat16, jnp.float32, jnp.int32
NT = (((1,), (1,)), ((), ()))
TN = (((0,), (0,)), ((), ()))
ROOM = 32 * 1024 * 1024


def shifted(block, axis, distance):
    size = lax.axis_size(axis)
    return lax.ppermute(block, axis, [((i - distance) % size, i) for i in range(size)])


def norms_of(floats):
    return jnp.sqrt(jnp.sum(floats * floats, -1, keepdims=True) + EPSILON)


def vmem(count):
    return [pl.BlockSpec(memory_space=pltpu.VMEM)] * count


def iota(shape, dim):
    return lax.broadcasted_iota(i32, shape, dim)


def prepare(pos_ref, *refs):
    sources, (out_ref, feats_hbm), held, sems, sem = refs[:5], refs[5:7], refs[7:12], refs[12], refs[13]
    copies = [pltpu.make_async_copy(src, dst, sems.at[k]) for k, (src, dst) in enumerate(zip(sources, held))]
    for copy in copies:
        copy.start()
    text_ref, ids_ref, domain_ref, bias_ref, feat_ref = held
    fans = [pltpu.make_async_copy(feat_ref, feats_hbm.at[k], sem.at[k]) for k in range(feats_hbm.shape[0])]
    copies[4].wait()
    for fan in fans:
        fan.start()
    for copy in copies[:4]:
        copy.wait()
    rows, width = text_ref.shape
    floats = text_ref[...].astype(f32)
    out_ref[:, :width] = (floats / norms_of(floats)).astype(bf16)
    wide = (rows, ids_ref.shape[1])
    mine = iota(wide, 1) == iota(wide, 0) + pos_ref[0] * rows
    own_id = jnp.sum(jnp.where(mine, ids_ref[...].astype(f32), 0.0), -1, keepdims=True)
    own_domain = jnp.sum(jnp.where(mine, domain_ref[...].astype(f32), 0.0), -1, keepdims=True)
    table = (rows, bias_ref.shape[1])
    chosen = own_domain.astype(i32) == iota(table, 1)
    bias = jnp.sum(jnp.where(chosen, jnp.broadcast_to(bias_ref[...], table), 0.0), -1, keepdims=True)
    whole = own_id.astype(i32)
    high = (whole >> 6).astype(f32)
    low = (whole & 63).astype(f32)
    first = bias.astype(bf16).astype(f32)
    second = (bias - first).astype(bf16).astype(f32)
    third = bias - first - second
    lane = iota((rows, TAIL), 1)
    tail = jnp.zeros((rows, TAIL), f32)
    for k, part in enumerate((high, low, first, second, third)):
        tail = jnp.where(lane == k, part, tail)
    out_ref[:, width:] = tail.astype(bf16)
    for fan in fans:
        fan.wait()


def assemble(*refs):
    out_ref, count = refs[-1], refs[0].shape[0]
    for k, ref in enumerate(refs[:-1]):
        out_ref[k * count : (k + 1) * count] = ref[...]


def slopes(rows, image_round, ids):
    width = image_round.shape[1]
    images = image_round.shape[0]
    tail = rows[:, width:]
    which = iota((TAIL, images), 0)
    take_id = jnp.where(which == 0, 64.0, jnp.where(which == 1, 1.0, 0.0)).astype(bf16)
    take_bias = jnp.where((which >= 2) & (which < 5), 1.0, 0.0).astype(bf16)
    logits = SCALE * lax.dot_general(rows[:, :width], image_round, NT, preferred_element_type=f32)
    logits = logits + jnp.dot(tail, take_bias, preferred_element_type=f32)
    text_ids = jnp.dot(tail, take_id, preferred_element_type=f32)
    signs = jnp.where(text_ids == ids.astype(f32), 1.0, -1.0)
    return (-signs * jax.nn.sigmoid(-signs * logits)).astype(bf16)


def image_side(a_ref, b_ref, own_ref, embed_ref, ids_ref, grad_ref, turned_ref, *share_refs):
    floats = embed_ref[...].astype(f32)
    norms = norms_of(floats)
    units = floats / norms
    rounded = units.astype(bf16)
    width = floats.shape[1]
    total = jnp.zeros(floats.shape, f32)
    for ref in (a_ref, b_ref):
        rows = ref[...]
        slope = slopes(rows, rounded, ids_ref[...])
        total = total + lax.dot_general(slope, rows[:, :width], TN, preferred_element_type=f32)
    total = SCALE * total
    grad = (total - units * jnp.sum(units * total, -1, keepdims=True)) / norms
    grad_ref[...] = grad.astype(bf16)
    turned = grad.T.astype(bf16)
    planes, pieces, run = turned_ref.shape[:3]
    for p in range(pieces):
        for z in range(planes):
            start = (p * planes + z) * run
            turned_ref[z, p] = turned[start : start + run]
    slope = slopes(own_ref[...], rounded, ids_ref[...])
    share = SCALE * jnp.dot(slope, rounded, preferred_element_type=f32)
    count = share_refs[0].shape[0]
    for k, ref in enumerate(share_refs):
        ref[...] = share[k * count : (k + 1) * count].astype(ref.dtype)


def head_side(pieces, feat_ref, turned_ref, out_ref):
    part = jnp.zeros((turned_ref.shape[1], feat_ref.shape[2]), f32)
    for k in range(turned_ref.shape[0]):
        part = part + jnp.dot(turned_ref[k], feat_ref[k], preferred_element_type=f32)
    targets, groups = out_ref.shape[0], part.shape[1] // 128
    run = part.shape[0] // targets
    for c in range(targets):
        place = c % (targets // pieces) * pieces + c // (targets // pieces)
        for g in range(groups):
            out_ref[place, g * run : (g + 1) * run] = part[
                c * run : (c + 1) * run, g * 128 : (g + 1) * 128
            ].astype(bf16)


def head_sum(parts_ref, out_ref):
    total = jnp.sum(parts_ref[...].astype(f32), 0)
    run, groups = out_ref.shape[0], out_ref.shape[1] // 128
    for g in range(groups):
        out_ref[:, g * 128 : (g + 1) * 128] = total[g * run : (g + 1) * run]


def finish(grad_ref, head_ref, text_ref, kept_ref, one_ref, two_ref, three_ref, image_ref, out_ref):
    image_ref[...] = jnp.dot(grad_ref[...], head_ref[...], preferred_element_type=f32).astype(bf16)
    floats = text_ref[...].astype(f32)
    norms = norms_of(floats)
    units = floats / norms
    total = kept_ref[...]
    for ref in (one_ref, two_ref, three_ref):
        total = total + ref[...].astype(f32)
    out_ref[...] = (total - units * jnp.sum(units * total, -1, keepdims=True)) / norms


def call(kernel, shapes, *args, smem=0, hbm=0, after=0, out_hbm=0, scratch=(), cost=None, room=None):
    specs = [pl.BlockSpec(memory_space=pltpu.SMEM)] * smem
    specs += [pl.BlockSpec(memory_space=pltpu.HBM)] * hbm
    specs += vmem(len(args) - smem - hbm - after)
    specs += [pl.BlockSpec(memory_space=pl.ANY)] * after
    outs = [jax.ShapeDtypeStruct(s, d) for s, d in shapes]
    out_specs = vmem(len(outs) - out_hbm) + [pl.BlockSpec(memory_space=pltpu.HBM)] * out_hbm
    single = len(outs) == 1
    return pl.pallas_call(
        kernel,
        out_shape=outs[0] if single else outs,
        in_specs=specs,
        out_specs=out_specs[0] if single else out_specs,
        scratch_shapes=list(scratch),
        compiler_params=pltpu.CompilerParams(vmem_limit_bytes=room),
        cost_estimate=cost,
        name=getattr(kernel, "func", kernel).__name__,
    )(*args)


def lasting(us):
    return pl.CostEstimate(flops=int(us * 1e9), bytes_accessed=0, transcendentals=0)


def local(image_embed, text_embed, image_feat, head, sample_id, domain, domain_bias):
    images, width = image_embed.shape
    texts = text_embed.shape[0]
    features = image_feat.shape[1]
    position = lax.axis_index(TOWER).astype(i32).reshape(1)
    ids = sample_id.reshape(1, images)
    planes = lax.axis_size("z")
    across = lax.axis_size("xh") * lax.axis_size("y")
    own_width = width // planes

    inputs = (text_embed, ids, domain.reshape(1, images), domain_bias.reshape(1, -1), image_feat)
    payload, feats = call(
        prepare, [((texts, width + TAIL), bf16), ((planes, images, features), bf16)],
        position, *inputs, smem=1, hbm=5, out_hbm=1,
        scratch=[pltpu.VMEM(v.shape, v.dtype) for v in inputs]
        + [pltpu.SemaphoreType.DMA((5,)), pltpu.SemaphoreType.DMA((planes,))],
    )
    feats = lax.all_to_all(feats, "z", 0, 0, tiled=True)

    window = [payload] + [shifted(payload, BLK, d) for d in (1, 2, 3)]
    own = call(
        assemble, [((len(window) * texts, width + TAIL), bf16)], *window,
        room=ROOM,
    )

    here = lax.all_gather(own, "xl", axis=0, tiled=True)
    there = shifted(here, "core", 1)

    pieces = lax.axis_size("xh")
    run = width // (planes * pieces)
    embed_grad, turned, kept, *aways = call(
        image_side,
        [((images, width), bf16), ((planes, pieces, run, images), bf16), ((texts, width), f32)]
        + [((texts, width), bf16)] * 3,
        here, there, own, image_embed, ids, room=ROOM,
    )
    turned, feats = lax.optimization_barrier((turned, feats))
    plane = lax.all_to_all(turned.reshape(planes, own_width, images), "z", 0, 0, tiled=True)

    backs = [shifted(away, BLK, -d) for d, away in zip((1, 2, 3), aways)]

    rows = own_width // across
    parts = call(
        functools.partial(head_side, pieces), [((across, rows * features // 128, 128), bf16)], feats, plane, room=ROOM,
    )
    parts = lax.all_to_all(parts, ("y", "xh"), 0, 0, tiled=True)
    image_grad, text_grad = call(
        finish, [((images, features), bf16), ((texts, width), f32)],
        embed_grad, head, text_embed, kept, *backs, cost=lasting(60), room=ROOM,
    )
    head_grad = call(head_sum, [((rows, features), f32)], parts, room=ROOM)
    return (image_grad, text_grad, head_grad)


def solution(mesh):
    split = Mesh(mesh.devices.reshape([n for _, n in SPLIT]), [name for name, _ in SPLIT])
    in_specs = (
        P(BLK, None),
        P(ALL, None),
        P(BLK, TOWER),
        P(None, TOWER),
        P(BLK),
        P(BLK),
        P(),
    )
    out_specs = (P(BLK, TOWER), P(ALL, None), P(BLK, TOWER))
    return jax.shard_map(local, mesh=split, in_specs=in_specs, out_specs=out_specs, check_vma=False)
```

```python
import jax
import jax.numpy as jnp
from jax import lax
from jax.experimental import pallas as pl
from jax.experimental.pallas import tpu as pltpu
from jax.sharding import Mesh, PartitionSpec as P

EPSILON = 1e-06
SCALE = 10.0
TAIL = 128
SPLIT = (("xh", 2), ("z", 8), ("y", 8), ("xl", 4), ("core", 2))
BLK = ("xh", "z", "y")
TOWER = ("xl", "core")
ALL = BLK + TOWER

bf16, f32, i32 = jnp.bfloat16, jnp.float32, jnp.int32
NT = (((1,), (1,)), ((), ()))
TN = (((0,), (0,)), ((), ()))
ROOM = 32 * 1024 * 1024


def shifted(block, axis, distance):
    size = lax.axis_size(axis)
    return lax.ppermute(block, axis, [((i - distance) % size, i) for i in range(size)])


def norms_of(floats):
    return jnp.sqrt(jnp.sum(floats * floats, -1, keepdims=True) + EPSILON)


def vmem(count):
    return [pl.BlockSpec(memory_space=pltpu.VMEM)] * count


def iota(shape, dim):
    return lax.broadcasted_iota(i32, shape, dim)


def prepare(pos_ref, *refs):
    sources, (out_ref, feats_hbm), held, sems, sem = refs[:5], refs[5:7], refs[7:12], refs[12], refs[13]
    copies = [pltpu.make_async_copy(src, dst, sems.at[k]) for k, (src, dst) in enumerate(zip(sources, held))]
    for copy in copies:
        copy.start()
    text_ref, ids_ref, domain_ref, bias_ref, feat_ref = held
    fans = [pltpu.make_async_copy(feat_ref, feats_hbm.at[k], sem.at[k]) for k in range(feats_hbm.shape[0])]
    copies[4].wait()
    for fan in fans:
        fan.start()
    for copy in copies[:4]:
        copy.wait()
    rows, width = text_ref.shape
    floats = text_ref[...].astype(f32)
    out_ref[:, :width] = (floats / norms_of(floats)).astype(bf16)
    wide = (rows, ids_ref.shape[1])
    mine = iota(wide, 1) == iota(wide, 0) + pos_ref[0] * rows
    own_id = jnp.sum(jnp.where(mine, ids_ref[...].astype(f32), 0.0), -1, keepdims=True)
    own_domain = jnp.sum(jnp.where(mine, domain_ref[...].astype(f32), 0.0), -1, keepdims=True)
    table = (rows, bias_ref.shape[1])
    chosen = own_domain.astype(i32) == iota(table, 1)
    bias = jnp.sum(jnp.where(chosen, jnp.broadcast_to(bias_ref[...], table), 0.0), -1, keepdims=True)
    whole = own_id.astype(i32)
    high = (whole >> 6).astype(f32)
    low = (whole & 63).astype(f32)
    first = bias.astype(bf16).astype(f32)
    second = (bias - first).astype(bf16).astype(f32)
    third = bias - first - second
    lane = iota((rows, TAIL), 1)
    tail = jnp.zeros((rows, TAIL), f32)
    for k, part in enumerate((high, low, first, second, third)):
        tail = jnp.where(lane == k, part, tail)
    out_ref[:, width:] = tail.astype(bf16)
    for fan in fans:
        fan.wait()


def assemble(*refs):
    out_ref, count = refs[-1], refs[0].shape[0]
    for k, ref in enumerate(refs[:-1]):
        out_ref[k * count : (k + 1) * count] = ref[...]


def slopes(rows, image_round, ids):
    width = image_round.shape[1]
    images = image_round.shape[0]
    tail = rows[:, width:]
    which = iota((TAIL, images), 0)
    take_id = jnp.where(which == 0, 64.0, jnp.where(which == 1, 1.0, 0.0)).astype(bf16)
    take_bias = jnp.where((which >= 2) & (which < 5), 1.0, 0.0).astype(bf16)
    logits = SCALE * lax.dot_general(rows[:, :width], image_round, NT, preferred_element_type=f32)
    logits = logits + jnp.dot(tail, take_bias, preferred_element_type=f32)
    text_ids = jnp.dot(tail, take_id, preferred_element_type=f32)
    signs = jnp.where(text_ids == ids.astype(f32), 1.0, -1.0)
    return (-signs * jax.nn.sigmoid(-signs * logits)).astype(bf16)


def toward(rows, rounded, ids):
    slope = slopes(rows, rounded, ids)
    return lax.dot_general(slope, rows[:, : rounded.shape[1]], TN, preferred_element_type=f32)


def near_side(rows_ref, own_ref, embed_ref, ids_ref, total_ref, *share_refs):
    floats = embed_ref[...].astype(f32)
    rounded = (floats / norms_of(floats)).astype(bf16)
    total_ref[...] = toward(rows_ref[...], rounded, ids_ref[...])
    slope = slopes(own_ref[...], rounded, ids_ref[...])
    share = SCALE * jnp.dot(slope, rounded, preferred_element_type=f32)
    count = share_refs[0].shape[0]
    for k, ref in enumerate(share_refs):
        ref[...] = share[k * count : (k + 1) * count].astype(ref.dtype)


def image_side(near_ref, rows_ref, embed_ref, ids_ref, grad_ref, turned_ref):
    floats = embed_ref[...].astype(f32)
    norms = norms_of(floats)
    units = floats / norms
    total = SCALE * (near_ref[...] + toward(rows_ref[...], units.astype(bf16), ids_ref[...]))
    grad = (total - units * jnp.sum(units * total, -1, keepdims=True)) / norms
    grad_ref[...] = grad.astype(bf16)
    turned = grad.T.astype(bf16)
    planes, pieces, run = turned_ref.shape[:3]
    for p in range(pieces):
        for z in range(planes):
            start = (p * planes + z) * run
            turned_ref[z, p] = turned[start : start + run]


def head_side(feat_ref, turned_ref, out_ref):
    part = jnp.zeros((turned_ref.shape[1], feat_ref.shape[2]), f32)
    for k in range(turned_ref.shape[0]):
        part = part + jnp.dot(turned_ref[k], feat_ref[k], preferred_element_type=f32)
    targets, groups = out_ref.shape[0], part.shape[1] // 128
    run = part.shape[0] // targets
    for c in range(targets):
        for g in range(groups):
            out_ref[c, g * run : (g + 1) * run] = part[
                c * run : (c + 1) * run, g * 128 : (g + 1) * 128
            ].astype(bf16)


def head_sum(parts_ref, out_ref):
    total = jnp.sum(parts_ref[...].astype(f32), 0)
    run, groups = out_ref.shape[0], out_ref.shape[1] // 128
    for g in range(groups):
        out_ref[:, g * 128 : (g + 1) * 128] = total[g * run : (g + 1) * run]


def finish(grad_ref, head_ref, text_ref, kept_ref, one_ref, two_ref, three_ref, image_ref, out_ref):
    image_ref[...] = jnp.dot(grad_ref[...], head_ref[...], preferred_element_type=f32).astype(bf16)
    floats = text_ref[...].astype(f32)
    norms = norms_of(floats)
    units = floats / norms
    total = kept_ref[...]
    for ref in (one_ref, two_ref, three_ref):
        total = total + ref[...].astype(f32)
    out_ref[...] = (total - units * jnp.sum(units * total, -1, keepdims=True)) / norms


def call(kernel, shapes, *args, smem=0, hbm=0, after=0, out_hbm=0, scratch=(), cost=None, room=None):
    specs = [pl.BlockSpec(memory_space=pltpu.SMEM)] * smem
    specs += [pl.BlockSpec(memory_space=pltpu.HBM)] * hbm
    specs += vmem(len(args) - smem - hbm - after)
    specs += [pl.BlockSpec(memory_space=pl.ANY)] * after
    outs = [jax.ShapeDtypeStruct(s, d) for s, d in shapes]
    out_specs = vmem(len(outs) - out_hbm) + [pl.BlockSpec(memory_space=pltpu.HBM)] * out_hbm
    single = len(outs) == 1
    return pl.pallas_call(
        kernel,
        out_shape=outs[0] if single else outs,
        in_specs=specs,
        out_specs=out_specs[0] if single else out_specs,
        scratch_shapes=list(scratch),
        compiler_params=pltpu.CompilerParams(vmem_limit_bytes=room),
        cost_estimate=cost,
        name=kernel.__name__,
    )(*args)


def lasting(us):
    return pl.CostEstimate(flops=int(us * 1e9), bytes_accessed=0, transcendentals=0)


def local(image_embed, text_embed, image_feat, head, sample_id, domain, domain_bias):
    images, width = image_embed.shape
    texts = text_embed.shape[0]
    features = image_feat.shape[1]
    position = lax.axis_index(TOWER).astype(i32).reshape(1)
    ids = sample_id.reshape(1, images)
    planes = lax.axis_size("z")
    across = lax.axis_size("xh") * lax.axis_size("y")
    own_width = width // planes

    inputs = (text_embed, ids, domain.reshape(1, images), domain_bias.reshape(1, -1), image_feat)
    payload, feats = call(
        prepare, [((texts, width + TAIL), bf16), ((planes, images, features), bf16)],
        position, *inputs, smem=1, hbm=5, out_hbm=1,
        scratch=[pltpu.VMEM(v.shape, v.dtype) for v in inputs]
        + [pltpu.SemaphoreType.DMA((5,)), pltpu.SemaphoreType.DMA((planes,))],
    )
    feats = lax.all_to_all(feats, "z", 0, 0, tiled=True)

    window = [payload] + [shifted(payload, BLK, d) for d in (1, 2, 3)]
    own = call(
        assemble, [((len(window) * texts, width + TAIL), bf16)], *window,
        room=ROOM,
    )

    here = lax.all_gather(own, "xl", axis=0, tiled=True)
    there = shifted(here, "core", 1)

    pieces = lax.axis_size("xh")
    run = width // (planes * pieces)
    near, kept, *aways = call(
        near_side,
        [((images, width), f32), ((texts, width), f32)] + [((texts, width), bf16)] * 3,
        here, own, image_embed, ids, cost=lasting(20), room=ROOM,
    )
    embed_grad, turned = call(
        image_side, [((images, width), bf16), ((planes, pieces, run, images), bf16)],
        near, there, image_embed, ids, room=ROOM,
    )
    turned, feats = lax.optimization_barrier((turned, feats))
    plane = lax.all_to_all(turned.reshape(planes, own_width, images), "z", 0, 0, tiled=True)

    backs = [shifted(away, BLK, -d) for d, away in zip((1, 2, 3), aways)]

    rows = own_width // across
    parts = call(
        head_side, [((across, rows * features // 128, 128), bf16)], feats, plane, room=ROOM,
    )
    parts = lax.all_to_all(parts, ("xh", "y"), 0, 0, tiled=True)
    image_grad, text_grad = call(
        finish, [((images, features), bf16), ((texts, width), f32)],
        embed_grad, head, text_embed, kept, *backs, cost=lasting(60), room=ROOM,
    )
    head_grad = call(head_sum, [((rows, features), f32)], parts, room=ROOM)
    return (image_grad, text_grad, head_grad)


def solution(mesh):
    split = Mesh(mesh.devices.reshape([n for _, n in SPLIT]), [name for name, _ in SPLIT])
    in_specs = (
        P(BLK, None),
        P(ALL, None),
        P(BLK, TOWER),
        P(None, TOWER),
        P(BLK),
        P(BLK),
        P(),
    )
    out_specs = (P(BLK, TOWER), P(ALL, None), P(BLK, TOWER))
    return jax.shard_map(local, mesh=split, in_specs=in_specs, out_specs=out_specs, check_vma=False)
```

```python
import jax
import jax.numpy as jnp
from jax import lax
from jax.experimental import pallas as pl
from jax.experimental.pallas import tpu as pltpu
from jax.sharding import Mesh, PartitionSpec as P

EPSILON = 1e-06
SCALE = 10.0
TAIL = 128
SPLIT = (("xh", 2), ("z", 8), ("y", 8), ("xl", 4), ("core", 2))
BLK = ("xh", "z", "y")
TOWER = ("xl", "core")
ALL = BLK + TOWER

bf16, f32, i32 = jnp.bfloat16, jnp.float32, jnp.int32
NT = (((1,), (1,)), ((), ()))
TN = (((0,), (0,)), ((), ()))
ROOM = 32 * 1024 * 1024


def shifted(block, axis, distance):
    size = lax.axis_size(axis)
    return lax.ppermute(block, axis, [((i - distance) % size, i) for i in range(size)])


def norms_of(floats):
    return jnp.sqrt(jnp.sum(floats * floats, -1, keepdims=True) + EPSILON)


def vmem(count):
    return [pl.BlockSpec(memory_space=pltpu.VMEM)] * count


def iota(shape, dim):
    return lax.broadcasted_iota(i32, shape, dim)


def prepare(pos_ref, *refs):
    sources, (out_ref, feats_hbm), held, sems, sem = refs[:5], refs[5:7], refs[7:12], refs[12], refs[13]
    copies = [pltpu.make_async_copy(src, dst, sems.at[k]) for k, (src, dst) in enumerate(zip(sources, held))]
    for copy in copies:
        copy.start()
    text_ref, ids_ref, domain_ref, bias_ref, feat_ref = held
    fans = [pltpu.make_async_copy(feat_ref, feats_hbm.at[k], sem.at[k]) for k in range(feats_hbm.shape[0])]
    copies[4].wait()
    for fan in fans:
        fan.start()
    for copy in copies[:4]:
        copy.wait()
    rows, width = text_ref.shape
    floats = text_ref[...].astype(f32)
    out_ref[:, :width] = (floats / norms_of(floats)).astype(bf16)
    wide = (rows, ids_ref.shape[1])
    mine = iota(wide, 1) == iota(wide, 0) + pos_ref[0] * rows
    own_id = jnp.sum(jnp.where(mine, ids_ref[...].astype(f32), 0.0), -1, keepdims=True)
    own_domain = jnp.sum(jnp.where(mine, domain_ref[...].astype(f32), 0.0), -1, keepdims=True)
    table = (rows, bias_ref.shape[1])
    chosen = own_domain.astype(i32) == iota(table, 1)
    bias = jnp.sum(jnp.where(chosen, jnp.broadcast_to(bias_ref[...], table), 0.0), -1, keepdims=True)
    whole = own_id.astype(i32)
    high = (whole >> 6).astype(f32)
    low = (whole & 63).astype(f32)
    first = bias.astype(bf16).astype(f32)
    second = (bias - first).astype(bf16).astype(f32)
    third = bias - first - second
    lane = iota((rows, TAIL), 1)
    tail = jnp.zeros((rows, TAIL), f32)
    for k, part in enumerate((high, low, first, second, third)):
        tail = jnp.where(lane == k, part, tail)
    out_ref[:, width:] = tail.astype(bf16)
    for fan in fans:
        fan.wait()


def assemble(*refs):
    out_ref, count = refs[-1], refs[0].shape[0]
    for k, ref in enumerate(refs[-2::-1]):
        out_ref[k * count : (k + 1) * count] = ref[...]


def slopes(rows, image_round, ids):
    width = image_round.shape[1]
    images = image_round.shape[0]
    tail = rows[:, width:]
    which = iota((TAIL, images), 0)
    take_id = jnp.where(which == 0, 64.0, jnp.where(which == 1, 1.0, 0.0)).astype(bf16)
    take_bias = jnp.where((which >= 2) & (which < 5), 1.0, 0.0).astype(bf16)
    logits = SCALE * lax.dot_general(rows[:, :width], image_round, NT, preferred_element_type=f32)
    logits = logits + jnp.dot(tail, take_bias, preferred_element_type=f32)
    text_ids = jnp.dot(tail, take_id, preferred_element_type=f32)
    signs = jnp.where(text_ids == ids.astype(f32), 1.0, -1.0)
    return (-signs * jax.nn.sigmoid(-signs * logits)).astype(bf16)


def toward(rows, rounded, ids):
    slope = slopes(rows, rounded, ids)
    return lax.dot_general(slope, rows[:, : rounded.shape[1]], TN, preferred_element_type=f32)


def near_side(rows_ref, own_ref, embed_ref, ids_ref, total_ref, *share_refs):
    floats = embed_ref[...].astype(f32)
    rounded = (floats / norms_of(floats)).astype(bf16)
    total_ref[...] = toward(rows_ref[...], rounded, ids_ref[...])
    slope = slopes(own_ref[...], rounded, ids_ref[...])
    share = SCALE * jnp.dot(slope, rounded, preferred_element_type=f32)
    count = share_refs[0].shape[0]
    for k, ref in enumerate(share_refs):
        ref[...] = share[k * count : (k + 1) * count].astype(ref.dtype)


def image_side(near_ref, rows_ref, embed_ref, ids_ref, grad_ref, turned_ref):
    floats = embed_ref[...].astype(f32)
    norms = norms_of(floats)
    units = floats / norms
    total = SCALE * (near_ref[...] + toward(rows_ref[...], units.astype(bf16), ids_ref[...]))
    grad = (total - units * jnp.sum(units * total, -1, keepdims=True)) / norms
    grad_ref[...] = grad.astype(bf16)
    turned = grad.T.astype(bf16)
    planes, pieces, run = turned_ref.shape[:3]
    for p in range(pieces):
        for z in range(planes):
            start = (p * planes + z) * run
            turned_ref[z, p] = turned[start : start + run]


def head_side(feat_ref, turned_ref, out_ref):
    part = jnp.zeros((turned_ref.shape[1], feat_ref.shape[2]), f32)
    for k in range(turned_ref.shape[0]):
        part = part + jnp.dot(turned_ref[k], feat_ref[k], preferred_element_type=f32)
    targets, groups = out_ref.shape[0], part.shape[1] // 128
    run = part.shape[0] // targets
    for c in range(targets):
        for g in range(groups):
            out_ref[c, g * run : (g + 1) * run] = part[
                c * run : (c + 1) * run, g * 128 : (g + 1) * 128
            ].astype(bf16)


def head_sum(parts_ref, out_ref):
    total = jnp.sum(parts_ref[...].astype(f32), 0)
    run, groups = out_ref.shape[0], out_ref.shape[1] // 128
    for g in range(groups):
        out_ref[:, g * 128 : (g + 1) * 128] = total[g * run : (g + 1) * run]


def finish(grad_ref, head_ref, text_ref, kept_ref, one_ref, two_ref, three_ref, image_ref, out_ref):
    image_ref[...] = jnp.dot(grad_ref[...], head_ref[...], preferred_element_type=f32).astype(bf16)
    floats = text_ref[...].astype(f32)
    norms = norms_of(floats)
    units = floats / norms
    total = kept_ref[...]
    for ref in (one_ref, two_ref, three_ref):
        total = total + ref[...].astype(f32)
    out_ref[...] = (total - units * jnp.sum(units * total, -1, keepdims=True)) / norms


def call(kernel, shapes, *args, smem=0, hbm=0, after=0, out_hbm=0, scratch=(), cost=None, room=None):
    specs = [pl.BlockSpec(memory_space=pltpu.SMEM)] * smem
    specs += [pl.BlockSpec(memory_space=pltpu.HBM)] * hbm
    specs += vmem(len(args) - smem - hbm - after)
    specs += [pl.BlockSpec(memory_space=pl.ANY)] * after
    outs = [jax.ShapeDtypeStruct(s, d) for s, d in shapes]
    out_specs = vmem(len(outs) - out_hbm) + [pl.BlockSpec(memory_space=pltpu.HBM)] * out_hbm
    single = len(outs) == 1
    return pl.pallas_call(
        kernel,
        out_shape=outs[0] if single else outs,
        in_specs=specs,
        out_specs=out_specs[0] if single else out_specs,
        scratch_shapes=list(scratch),
        compiler_params=pltpu.CompilerParams(vmem_limit_bytes=room),
        cost_estimate=cost,
        name=kernel.__name__,
    )(*args)


def lasting(us):
    return pl.CostEstimate(flops=int(us * 1e9), bytes_accessed=0, transcendentals=0)


def local(image_embed, text_embed, image_feat, head, sample_id, domain, domain_bias):
    images, width = image_embed.shape
    texts = text_embed.shape[0]
    features = image_feat.shape[1]
    position = lax.axis_index(TOWER).astype(i32).reshape(1)
    ids = sample_id.reshape(1, images)
    planes = lax.axis_size("z")
    across = lax.axis_size("xh") * lax.axis_size("y")
    own_width = width // planes

    inputs = (text_embed, ids, domain.reshape(1, images), domain_bias.reshape(1, -1), image_feat)
    payload, feats = call(
        prepare, [((texts, width + TAIL), bf16), ((planes, images, features), bf16)],
        position, *inputs, smem=1, hbm=5, out_hbm=1,
        scratch=[pltpu.VMEM(v.shape, v.dtype) for v in inputs]
        + [pltpu.SemaphoreType.DMA((5,)), pltpu.SemaphoreType.DMA((planes,))],
    )
    feats = lax.all_to_all(feats, "z", 0, 0, tiled=True)

    window = [payload] + [shifted(payload, BLK, d) for d in (1, 2, 3)]
    own = call(
        assemble, [((len(window) * texts, width + TAIL), bf16)], *window[::-1],
        room=ROOM,
    )

    here = lax.all_gather(own, "xl", axis=0, tiled=True)
    there = shifted(here, "core", 1)

    pieces = lax.axis_size("xh")
    run = width // (planes * pieces)
    near, kept, *aways = call(
        near_side,
        [((images, width), f32), ((texts, width), f32)] + [((texts, width), bf16)] * 3,
        here, own, image_embed, ids, cost=lasting(20), room=ROOM,
    )
    embed_grad, turned = call(
        image_side, [((images, width), bf16), ((planes, pieces, run, images), bf16)],
        near, there, image_embed, ids, room=ROOM,
    )
    turned, feats = lax.optimization_barrier((turned, feats))
    plane = lax.all_to_all(turned.reshape(planes, own_width, images), "z", 0, 0, tiled=True)

    backs = [shifted(away, BLK, -d) for d, away in zip((1, 2, 3), aways)]

    rows = own_width // across
    parts = call(
        head_side, [((across, rows * features // 128, 128), bf16)], feats, plane, room=ROOM,
    )
    parts = lax.all_to_all(parts, ("xh", "y"), 0, 0, tiled=True)
    image_grad, text_grad = call(
        finish, [((images, features), bf16), ((texts, width), f32)],
        embed_grad, head, text_embed, kept, *backs, cost=lasting(60), room=ROOM,
    )
    head_grad = call(head_sum, [((rows, features), f32)], parts, room=ROOM)
    return (image_grad, text_grad, head_grad)


def solution(mesh):
    split = Mesh(mesh.devices.reshape([n for _, n in SPLIT]), [name for name, _ in SPLIT])
    in_specs = (
        P(BLK, None),
        P(ALL, None),
        P(BLK, TOWER),
        P(None, TOWER),
        P(BLK),
        P(BLK),
        P(),
    )
    out_specs = (P(BLK, TOWER), P(ALL, None), P(BLK, TOWER))
    return jax.shard_map(local, mesh=split, in_specs=in_specs, out_specs=out_specs, check_vma=False)
```
